512 devices in a mesh: row: 32 (over x, z_lo, core), col: 16 (over z_hi, y).
Axes of the slice: x: 4, y: 4, z: 16 (z_hi: 4, z_lo: 4; z = z_hi * 4 + z_lo), core: 2. Of those that a mesh axis runs over, the one named last changes fastest.
Arguments:
- solution: float32 [8, 2048, 2048], P(None, 'row', 'col'), may hold values from -1 to 1, as said below
- search: float32 [8, 2048, 2048], P(None, 'row', 'col'), may hold values from -1 to 1, as said below
- basis: float32 [8, 2048, 2048], P(None, 'row', 'col'), may hold values from -1 to 1, as said below
- resid_a: float32 [2048, 2048], P('row', 'col'), may hold values from -1 to 1, as said below
- resid_b: float32 [2048, 2048], P('row', 'col'), may hold values from -1 to 1, as said below
- scalars: float32 [3], replicated, may hold values from 0.5 to 2
- profile_a: float32 [8, 512], replicated, may hold values from -0.25 to 0.25
- profile_b: float32 [8, 512], replicated, may hold values from -0.25 to 0.25
- source_mask: int32 [2048, 2048], P('row', 'col'), may hold values 0 or 1
- weight_code: int32 [2048, 2048], P('row', 'col'), may hold values from 0 to 7
- roll_code: int32 [2048, 2048], P('row', 'col'), may hold values from 0 to 2
Outputs:
- next_solution: float32 [8, 2048, 2048], P(None, 'row', 'col')
- next_search: float32 [8, 2048, 2048], P(None, 'row', 'col')
- next_basis: float32 [8, 2048, 2048], P(None, 'row', 'col')
- next_resid_a: float32 [2048, 2048], P('row', 'col')
- next_resid_b: float32 [2048, 2048], P('row', 'col')
The draws below stay inside these ranges and needn't reach their ends.
Inputs may be any that keep to these rules, and one draw needn't show every extreme that they name: `solution`: the whole array has Euclidean norm 1. `search`: the whole array has Euclidean norm 1. `basis`: the whole array has Euclidean norm 1. Euclidean norm sqrt(1/2), so that resid_a and resid_b together have norm 1. Euclidean norm sqrt(1/2), so that resid_a and resid_b together have norm 1.
All inputs are finite; a program needn't handle non-finite values. No bound on the sum of `source_mask` on one device may be relied on, other than what follows from the above.
Results may differ from the reference program's by a relative error of at most 0.000078.
Values sent between devices are 32-bit elements; how exact they have to be, the bound alone decides.
A program may use at most 64 MiB of HBM per device.

```python
import jax
import jax.numpy as jnp
from jax import lax

K = 8
L = 512
NC = 2048
NR = 2048


def normed_field(key, shape, norm_value):
    values = jax.random.normal(key, shape, jnp.float32)
    return values * (norm_value / jnp.sqrt(jnp.sum(values * values)))


def draw_solution(key, part):
    return normed_field(jax.random.fold_in(key, 11), (K, NR, NC), 1.0)


def draw_search(key, part):
    return normed_field(jax.random.fold_in(key, 23), (K, NR, NC), 1.0)


def draw_basis(key, part):
    return normed_field(jax.random.fold_in(key, 37), (K, NR, NC), 1.0)


def draw_resid_a(key, part):
    return normed_field(jax.random.fold_in(key, 41), (NR, NC), 0.5 ** 0.5)


def draw_resid_b(key, part):
    return normed_field(jax.random.fold_in(key, 53), (NR, NC), 0.5 ** 0.5)


def plant(entries, stream_key, smallest, largest):
    extent = entries.shape
    place = [jax.random.randint(jax.random.fold_in(stream_key, axis), (), 0, extent[axis]) for axis in range(len(extent))]
    entries = entries.at[tuple(place)].set(smallest)
    longest = extent.index(max(extent))
    place[longest] = (place[longest] + 1) % extent[longest]
    return entries.at[tuple(place)].set(largest)


def gaussian(own_key, extent, spread, limit, dtype=jnp.bfloat16):
    entries = jax.random.normal(own_key, extent, jnp.float32) * spread
    return jnp.minimum(jnp.maximum(entries, -limit), limit).astype(dtype)


def setup_inputs(seed: int = 0) -> dict:
    splits = jax.random.split(jax.random.key(seed), 12)
    solution = draw_solution(jax.random.fold_in(splits[11], 71), 0)
    search = draw_search(jax.random.fold_in(splits[11], 71), 0)
    basis = draw_basis(jax.random.fold_in(splits[11], 71), 0)
    resid_a = draw_resid_a(jax.random.fold_in(splits[11], 71), 0)
    resid_b = draw_resid_b(jax.random.fold_in(splits[11], 71), 0)
    scalars = jnp.clip(jax.random.uniform(splits[5], (3,), jnp.float32, 0.5, 2.0), 0.5, 2.0)
    profile_a = gaussian(splits[6], (K, L), L ** -0.5, 0.25, jnp.float32)
    profile_b = gaussian(splits[7], (K, L), L ** -0.5, 0.25, jnp.float32)
    source_mask = plant((jax.random.randint(splits[8], (NR, NC), 0, 4) < 3).astype(jnp.int32), jax.random.fold_in(splits[8], 1), 0, 1)
    weight_code = plant(jax.random.randint(splits[9], (NR, NC), 0, 8), jax.random.fold_in(splits[9], 1), 0, 7).astype(jnp.int32)
    roll_code = plant(jax.random.randint(splits[10], (NR, NC), 0, 3), jax.random.fold_in(splits[10], 1), 0, 2).astype(jnp.int32)
    return {"solution": solution, "search": search, "basis": basis, "resid_a": resid_a, "resid_b": resid_b, "scalars": scalars, "profile_a": profile_a, "profile_b": profile_b, "source_mask": source_mask, "weight_code": weight_code, "roll_code": roll_code}


epsilon = 1e-12

def roll_weights(weight_code, roll_code):
    base = 1.0 / (1.0 + 0.25 * weight_code.astype(jnp.float32))
    return (base * (roll_code != 2).astype(jnp.float32), base * (roll_code != 1).astype(jnp.float32))

def forward(maps, masked, weight_a, weight_b, profile_a, profile_b):
    source = maps * masked[None]
    length = profile_a.shape[1]
    rows_all = source.shape[1]
    cols_all = source.shape[2]
    total = cols_all + length
    spectrum = jnp.fft.rfft(source, n=total, axis=2)
    kernel = jnp.fft.rfft(profile_a, n=total, axis=1)
    image_a = jnp.fft.irfft(lax.optimization_barrier(jnp.sum(spectrum * kernel[:, None, :], axis=0)), n=total, axis=1)[:, :cols_all]
    total = rows_all + length
    spectrum = jnp.fft.rfft(source, n=total, axis=1)
    kernel = jnp.fft.rfft(profile_b, n=total, axis=1)
    image_b = jnp.fft.irfft(lax.optimization_barrier(jnp.sum(spectrum * kernel[:, :, None], axis=0)), n=total, axis=0)[:rows_all]
    return (weight_a * image_a, weight_b * image_b)

def adjoint(first, second, masked, weight_a, weight_b, profile_a, profile_b):
    length = profile_a.shape[1]
    rows_all, cols_all = first.shape
    total = cols_all + length
    spectrum = jnp.fft.rfft(weight_a * first, n=total, axis=1)
    kernel = jnp.conj(jnp.fft.rfft(profile_a, n=total, axis=1))
    grad_a = jnp.fft.irfft(spectrum[None] * kernel[:, None, :], n=total, axis=2)[:, :, :cols_all]
    total = rows_all + length
    spectrum = jnp.fft.rfft(weight_b * second, n=total, axis=0)
    kernel = jnp.conj(jnp.fft.rfft(profile_b, n=total, axis=1))
    grad_b = jnp.fft.irfft(spectrum[None] * kernel[:, :, None], n=total, axis=1)[:, :rows_all]
    return masked[None] * (grad_a + grad_b)

def reference(solution, search, basis, resid_a, resid_b, scalars, profile_a, profile_b, source_mask, weight_code, roll_code):
    alpha = scalars[0]
    phibar = scalars[1]
    rhobar = scalars[2]
    weight_a, weight_b = roll_weights(weight_code, roll_code)
    masked = source_mask.astype(jnp.float32)
    image_a, image_b = forward(basis, masked, weight_a, weight_b, profile_a, profile_b)
    raw_a = image_a - alpha * resid_a
    raw_b = image_b - alpha * resid_b
    beta = jnp.sqrt(jnp.sum(raw_a * raw_a) + jnp.sum(raw_b * raw_b) + epsilon)
    next_resid_a = raw_a / beta
    next_resid_b = raw_b / beta
    raw_v = adjoint(next_resid_a, next_resid_b, masked, weight_a, weight_b, profile_a, profile_b) - beta * basis
    alpha_next = jnp.sqrt(jnp.sum(raw_v * raw_v) + epsilon)
    next_basis = raw_v / alpha_next
    rho_total = jnp.sqrt(rhobar * rhobar + beta * beta)
    cosine = rhobar / rho_total
    sine = beta / rho_total
    theta = sine * alpha_next
    phi_value = cosine * phibar
    next_solution = solution + phi_value / rho_total * search
    next_search = next_basis - theta / rho_total * search
    return (next_solution, next_search, next_basis, next_resid_a, next_resid_b)
```

```python
import functools

import jax
import jax.numpy as jnp
from jax import lax
from jax.experimental import pallas as pl
from jax.experimental.pallas import tpu as pltpu
from jax.sharding import Mesh
from jax.sharding import PartitionSpec as P

X, Z, C, H, Y = "row_0", "row_1", "row_2", "col_0", "col_1"
ROW = (X, Z, C)
COL = (H, Y)
MESH = pl.DeviceIdType.MESH
f32 = jnp.float32
bf16 = jnp.bfloat16
EPS = 1e-12

K, L, R, W = 8, 512, 64, 128
CL = 5
EXT = CL * W

NEAR = [(dz, dc) for dz in range(4) for dc in range(2)][1:]
PLANE = [(dx, dy) for dx in range(4) for dy in range(4)][1:]
FAR = [1, 2, 3]


def split(x):
    hi = x.astype(bf16)
    return hi, (x - hi.astype(f32)).astype(bf16)


def dot(a, b, ca, cb):
    return lax.dot_general(a, b, (((ca,), (cb,)), ((), ())), preferred_element_type=f32)


def kernel(
    basis, resid_a, resid_b, scal, pa, pb, mask, wcode, rcode,
    raw_v, raw_a, raw_b, coef,
    src_r, src_c, ta_hi, ta_lo, tb_hi, tb_lo, wext_a, wext_b,
    even, odd, r1, r2, r3, cp, c1, c2, ext_c, ext_e, ext_o,
    own, g_near, g_plane, g_far, send_sem, recv_sem,
):
    x, z, c, h, y = (lax.axis_index(a) for a in (X, Z, C, H, Y))
    started = []

    def near(o):
        return {Z: lax.rem(z + o[0], 4), C: lax.rem(c + o[1], 2)}

    def plane(o):
        return {X: lax.rem(x + o[0], 4), Y: lax.rem(y + o[1], 4)}

    def far(o):
        return {H: lax.rem(h + o, 4)}

    def copy(src, dst, to, again=False):
        i = len(started) - again
        d = pltpu.make_async_remote_copy(
            src_ref=src, dst_ref=dst, send_sem=send_sem.at[i], recv_sem=recv_sem.at[i], device_id=to, device_id_type=MESH
        )
        if not again:
            started.append(d)
        return d

    barrier = pltpu.get_barrier_semaphore()
    peers = [near(o) for o in NEAR] + [plane(o) for o in PLANE] + [far(o) for o in FAR]
    for to in peers:
        pl.semaphore_signal(barrier, inc=1, device_id=to, device_id_type=MESH)

    m = mask[...].astype(f32)
    pad = jnp.zeros((1, EXT - L), f32)
    for k in range(K):
        hi, lo = split(basis[k] * m)
        src_r[0:R, k * W : (k + 1) * W] = hi
        src_r[R : 2 * R, k * W : (k + 1) * W] = lo
        src_c[k * R : (k + 1) * R, 0:W] = hi
        src_c[k * R : (k + 1) * R, W : 2 * W] = lo
        row = jnp.concatenate([pb[k : k + 1, :], pad], axis=1)
        t = pltpu.roll(jnp.broadcast_to(row, (R, EXT)), 0, 1, stride=1, stride_axis=0)
        hi, lo = split(t)
        tb_hi[k * R : (k + 1) * R, :] = hi
        tb_lo[k * R : (k + 1) * R, :] = lo
    part = dot(tb_hi[...], src_c[...], 0, 0) + dot(tb_lo[...], src_c[...], 0, 0)
    part = part[:, :W] + part[:, W:]
    for level in range(9):
        block = part[level * R : (level + 1) * R]
        if level % 2:
            odd[level // 2] = block
        else:
            even[level // 2] = block

    pl.semaphore_wait(barrier, len(peers))
    to_core = near((0, 1))
    s_r1 = copy(odd, r1, to_core)
    s_r1.start()

    for k in range(K):
        row = jnp.concatenate([pa[k : k + 1, :], pad], axis=1)
        t = pltpu.roll(jnp.broadcast_to(row, (W, EXT)), 0, 1, stride=1, stride_axis=0)
        hi, lo = split(t)
        ta_hi[k * W : (k + 1) * W, :] = hi
        ta_lo[k * W : (k + 1) * W, :] = lo
    part = dot(src_r[...], ta_hi[...], 1, 0) + dot(src_r[...], ta_lo[...], 1, 0)
    part = part[:R] + part[R:]
    for level in range(CL):
        cp[level] = part[:, level * W : (level + 1) * W]
    s_c1 = [copy(cp.at[d], c1.at[d], plane((0, d))) for d in (1, 2, 3)]
    for s in s_c1:
        s.start()

    s_r1.wait_recv()
    for i in range(4):
        even[1 - c + i] = even[1 - c + i] + r1[i]
    s_r2 = [copy(even.at[d], r2.at[d], near((d, 0))) for d in (1, 2, 3)]
    for s in s_r2:
        s.start()

    for s in s_c1:
        s.wait_recv()
    here, there = cp[0], cp[4]
    for d in (1, 2, 3):
        mine = d <= y
        here = here + jnp.where(mine, c1[d], 0.0)
        there = there + jnp.where(mine, 0.0, c1[d])
    cp[4] = there
    s_c2 = copy(cp.at[4], c2, far(1))
    s_c2.start()

    for s in s_r2:
        s.wait_recv()
    rows_here, there = even[0], even[4]
    for d in (1, 2, 3):
        mine = d <= z
        rows_here = rows_here + jnp.where(mine, r2[d], 0.0)
        there = there + jnp.where(mine, 0.0, r2[d])
    even[4] = there
    s_r3 = copy(even.at[4], r3, plane((1, 0)))
    s_r3.start()

    alpha = scal[0]
    base = 1.0 / (1.0 + 0.25 * wcode[...].astype(f32))
    weight_a = jnp.where(rcode[...] != 2, base, 0.0)
    weight_b = jnp.where(rcode[...] != 1, base, 0.0)

    s_c2.wait_recv()
    image = here + jnp.where(h > 0, c2[...], 0.0)
    ra = weight_a * image - alpha * resid_a[...]
    raw_a[...] = ra
    wa = weight_a * ra
    ext_c[0] = wa
    s_d1 = copy(ext_c.at[0], ext_c.at[4], far(3))
    s_d1.start()
    s_d2 = []
    for d in (1, 2, 3):
        to = plane((0, d))
        s = copy(ext_c.at[0], ext_c.at[4 - d], to)
        later = copy(ext_c.at[4], ext_c.at[4 - d], to, again=True)
        s_d2.append((s, later, y + d >= 4))
    for s, later, now in s_d2:
        pl.when(now)(s.start)

    s_r3.wait_recv()
    image = rows_here + jnp.where(x > 0, r3[...], 0.0)
    rb = weight_b * image - alpha * resid_b[...]
    raw_b[...] = rb
    wb = weight_b * rb
    ext_e[0] = wb
    s_a1 = copy(ext_e.at[0], ext_e.at[4], plane((3, 0)))
    s_a1.start()
    s_a2 = []
    for d in (1, 2, 3):
        to = near((d, 0))
        s = copy(ext_e.at[0], ext_e.at[4 - d], to)
        later = copy(ext_e.at[4], ext_e.at[4 - d], to, again=True)
        s_a2.append((s, later, z + d >= 4))
    for s, later, now in s_a2:
        pl.when(now)(s.start)

    def begin(n, tile):
        own[n, 0] = tile
        out = [copy(own.at[n, 0], g_near.at[n, i], near(o)) for i, o in enumerate(NEAR)]
        for s in out:
            s.start()
        return out

    def middle(n, out):
        for s in out:
            s.wait_recv()
        tile = own[n, 0]
        for i in range(len(NEAR)):
            tile = tile + g_near[n, i]
        own[n, 1] = tile
        out = [copy(own.at[n, 1], g_plane.at[n, i], plane(o)) for i, o in enumerate(PLANE)]
        for s in out:
            s.start()
        return out

    def last(n, out):
        for s in out:
            s.wait_recv()
        tile = own[n, 1]
        for i in range(len(PLANE)):
            tile = tile + g_plane[n, i]
        own[n, 2] = tile
        out = [copy(own.at[n, 2], g_far.at[n, i], far(o)) for i, o in enumerate(FAR)]
        for s in out:
            s.start()
        return out

    def total(n, out):
        for s in out:
            s.wait_recv()
        tile = own[n, 2]
        for i in range(len(FAR)):
            tile = tile + g_far[n, i]
        return jnp.sum(jnp.sum(tile, axis=1, keepdims=True), axis=0, keepdims=True)

    sq = ra * ra + rb * rb
    out = begin(0, jnp.sum(sq.reshape(R // 8, 8, W), axis=0))

    s_d1.wait_recv()
    ext_c[4] = jnp.where(h < 3, ext_c[4], 0.0)
    for s, later, now in s_d2:
        pl.when(jnp.logical_not(now))(later.start)
    s_a1.wait_recv()
    ext_e[4] = jnp.where(x < 3, ext_e[4], 0.0)
    for s, later, now in s_a2:
        pl.when(jnp.logical_not(now))(later.start)

    def put_a(level, block):
        hi, lo = split(block)
        wext_a[0:R, level * W : (level + 1) * W] = hi
        wext_a[R : 2 * R, level * W : (level + 1) * W] = lo

    def put_b(level, block):
        hi, lo = split(block)
        wext_b[level * R : (level + 1) * R, 0:W] = hi
        wext_b[level * R : (level + 1) * R, W : 2 * W] = lo

    put_a(0, wa)
    put_a(4, ext_c[4])
    put_b(0, wb)
    put_b(8, ext_e[4])
    put_b(9, jnp.zeros((R, W), f32))
    out = middle(0, out)

    for s, _, _ in s_a2:
        s.wait_recv()
    s_a3 = copy(ext_e.at[pl.ds(1 - c, 4)], ext_o, to_core)
    s_a3.start()
    for d in (1, 2, 3):
        put_b(2 * d, ext_e[d])
    for s, _, _ in s_d2:
        s.wait_recv()
    for d in (1, 2, 3):
        put_a(d, ext_c[d])
    ga = dot(wext_a[...], ta_hi[...], 1, 1) + dot(wext_a[...], ta_lo[...], 1, 1)
    ga = ga[:R] + ga[R:]
    for k in range(K):
        raw_v[k] = ga[:, k * W : (k + 1) * W]
    out = last(0, out)
    s_a3.wait_recv()
    for d in range(4):
        put_b(2 * d + 1, ext_o[d])
    gb = dot(tb_hi[...], wext_b[...], 1, 0) + dot(tb_lo[...], wext_b[...], 1, 0)
    gb = gb[:, :W] + gb[:, W:]
    beta = jnp.sqrt(total(0, out) + EPS)
    inv_beta = 1.0 / beta
    scaled = m * inv_beta
    sq = jnp.zeros((R, W), f32)
    for k in range(K):
        v = scaled * (raw_v[k] + gb[k * R : (k + 1) * R]) - beta * basis[k]
        raw_v[k] = v
        sq = sq + v * v
    out = begin(1, jnp.sum(sq.reshape(R // 8, 8, W), axis=0))
    out = middle(1, out)
    out = last(1, out)
    alpha_next = jnp.sqrt(total(1, out) + EPS)
    phibar, rhobar = scal[1], scal[2]
    rho = jnp.sqrt(rhobar * rhobar + beta * beta)
    cosine = rhobar / rho
    sine = beta / rho
    theta = sine * alpha_next
    phi = cosine * phibar
    for i, value in enumerate((inv_beta, 1.0 / alpha_next, phi / rho, theta / rho)):
        coef[i : i + 1, :] = jnp.broadcast_to(value, (1, W))
    coef[4:8, :] = jnp.zeros((4, W), f32)
    for s in started:
        s.wait_send()


N_COPIES = 18 + 2 * (len(NEAR) + len(PLANE) + len(FAR))


def finish(raw_v, raw_a, raw_b, coef, sol, search, sol_o, search_o, basis_o, resid_a, resid_b):
    inv_beta, inv_alpha = coef[0:1, :], coef[1:2, :]
    step, turn = coef[2:3, :], coef[3:4, :]
    w = search[...]
    v = raw_v[...] * inv_alpha
    sol_o[...] = sol[...] + step * w
    basis_o[...] = v
    search_o[...] = v - turn * w
    resid_a[...] = raw_a[...] * inv_beta
    resid_b[...] = raw_b[...] * inv_beta


def body(sol, search, basis, resid_a, resid_b, scal, pa, pb, mask, wcode, rcode):
    vmem = pl.BlockSpec(memory_space=pltpu.VMEM)
    smem = pl.BlockSpec(memory_space=pltpu.SMEM)
    image = jax.ShapeDtypeStruct((R, W), f32)
    maps = jax.ShapeDtypeStruct((K, R, W), f32)
    raw_v, raw_a, raw_b, coef = pl.pallas_call(
        kernel,
        out_shape=(maps, image, image, jax.ShapeDtypeStruct((8, W), f32)),
        in_specs=[vmem, vmem, vmem, smem, vmem, vmem, vmem, vmem, vmem],
        out_specs=(vmem, vmem, vmem, vmem),
        scratch_shapes=[
            pltpu.VMEM((2 * R, K * W), bf16),
            pltpu.VMEM((K * R, 2 * W), bf16),
            pltpu.VMEM((K * W, EXT), bf16),
            pltpu.VMEM((K * W, EXT), bf16),
            pltpu.VMEM((K * R, EXT), bf16),
            pltpu.VMEM((K * R, EXT), bf16),
            pltpu.VMEM((2 * R, EXT), bf16),
            pltpu.VMEM((EXT, 2 * W), bf16),
            pltpu.VMEM((5, R, W), f32),
            pltpu.VMEM((4, R, W), f32),
            pltpu.VMEM((4, R, W), f32),
            pltpu.VMEM((4, R, W), f32),
            pltpu.VMEM((R, W), f32),
            pltpu.VMEM((5, R, W), f32),
            pltpu.VMEM((4, R, W), f32),
            pltpu.VMEM((R, W), f32),
            pltpu.VMEM((5, R, W), f32),
            pltpu.VMEM((5, R, W), f32),
            pltpu.VMEM((4, R, W), f32),
            pltpu.VMEM((2, 3, 8, W), f32),
            pltpu.VMEM((2, len(NEAR), 8, W), f32),
            pltpu.VMEM((2, len(PLANE), 8, W), f32),
            pltpu.VMEM((2, len(FAR), 8, W), f32),
            pltpu.SemaphoreType.DMA((N_COPIES,)),
            pltpu.SemaphoreType.DMA((N_COPIES,)),
        ],
        compiler_params=pltpu.CompilerParams(
            collective_id=0, has_side_effects=True, vmem_limit_bytes=48 * 1024 * 1024
        ),
    )(basis, resid_a, resid_b, scal, pa, pb, mask, wcode, rcode)
    return pl.pallas_call(
        finish,
        out_shape=(maps, maps, maps, image, image),
        in_specs=[vmem] * 6,
        out_specs=(vmem,) * 5,
        compiler_params=pltpu.CompilerParams(vmem_limit_bytes=16 * 1024 * 1024),
    )(raw_v, raw_a, raw_b, coef, sol, search)


def solution(mesh):
    torus = Mesh(mesh.devices.reshape(4, 4, 2, 4, 4), (X, Z, C, H, Y))
    maps, image = P(None, ROW, COL), P(ROW, COL)
    return jax.shard_map(
        body,
        mesh=torus,
        in_specs=(maps, maps, maps, image, image, P(), P(), P(), image, image, image),
        out_specs=(maps, maps, maps, image, image),
        check_vma=False,
    )
```

```python
import jax
import jax.numpy as jnp
from jax import lax
from jax.experimental import pallas as pl
from jax.experimental.pallas import tpu as pltpu
from jax.sharding import Mesh
from jax.sharding import PartitionSpec as P

X, Z, C, H, Y = "row_0", "row_1", "row_2", "col_0", "col_1"
ROW = (X, Z, C)
COL = (H, Y)
MESH = pl.DeviceIdType.MESH
f32 = jnp.float32
bf16 = jnp.bfloat16
EPS = 1e-12

K, L, R, W = 8, 512, 64, 128
CL = 5
EXT = CL * W


def ring(a, n):
    return min(a, n - a)


PLANE = [(dx, dy, dc) for dx in range(4) for dy in range(4) for dc in range(2)][1:]
PLANE.sort(key=lambda o: -(ring(o[0], 4) + ring(o[1], 4)))
LINE = sorted(range(1, 16), key=lambda d: -ring(d, 16))


def split(x):
    hi = x.astype(bf16)
    return hi, (x - hi.astype(f32)).astype(bf16)


def dot(a, b, ca, cb):
    return lax.dot_general(a, b, (((ca,), (cb,)), ((), ())), preferred_element_type=f32)


def kernel(
    basis_h, resid_a_h, resid_b_h, scal_h, pa_h, pb_h, mask_h, wcode_h, rcode_h,
    raw_v_h, raw_a_h, raw_b_h, coef_h,
    raw_v, raw_a, raw_b, coef, basis, resid_a, resid_b, scal, pa, pb, mask, wcode, rcode,
    src_r, src_c, ta_hi, ta_lo, tb_hi, tb_lo, wext_a, wext_b,
    even, odd, r1, r2, r3, cp, c1, c2, ext_c, ext_e, ext_o,
    sums_plane, sums_line, send_sem, recv_sem, load_sem,
):
    x, z, c, h, y = (lax.axis_index(a) for a in (X, Z, C, H, Y))
    started = []

    def core():
        return {C: 1 - c}

    def run(d):
        return {Z: lax.rem(z + d, 4)}

    def along_x(d):
        return {X: lax.rem(x + d, 4)}

    def along_y(d):
        return {Y: lax.rem(y + d, 4)}

    def far(d):
        return {H: lax.rem(h + d, 4)}

    def plane(o):
        return {X: lax.rem(x + o[0], 4), Y: lax.rem(y + o[1], 4), C: lax.rem(c + o[2], 2)}

    def line(d):
        at = 4 * h + z + d
        return {H: lax.rem(at // 4, 4), Z: lax.rem(at, 4)}

    def copy(src, dst, to, again=False):
        i = len(started) - again
        d = pltpu.make_async_remote_copy(
            src_ref=src, dst_ref=dst, send_sem=send_sem.at[i], recv_sem=recv_sem.at[i], device_id=to, device_id_type=MESH
        )
        if not again:
            started.append(d)
        return d

    barrier = pltpu.get_barrier_semaphore()
    peers = [core()] + [run(d) for d in (1, 2, 3)] + [along_y(d) for d in (1, 2, 3)]
    peers += [along_x(1), along_x(3), far(1), far(3)]
    for to in peers:
        pl.semaphore_signal(barrier, inc=1, device_id=to, device_id_type=MESH)

    pairs = (
        (pa_h, pa), (pb_h, pb), (mask_h, mask), (basis_h, basis), (scal_h, scal), (wcode_h, wcode),
        (rcode_h, rcode), (resid_a_h, resid_a), (resid_b_h, resid_b),
    )
    loads = [pltpu.make_async_copy(a, b, load_sem.at[i]) for i, (a, b) in enumerate(pairs)]
    for s in loads:
        s.start()

    pad = jnp.zeros((1, EXT - L), f32)

    def table(profile, k, rows):
        row = jnp.concatenate([profile[k : k + 1, :], pad], axis=1)
        return split(pltpu.roll(jnp.broadcast_to(row, (rows, EXT)), 0, 1, stride=1, stride_axis=0))

    loads[0].wait()
    for k in range(K):
        ta_hi[k * W : (k + 1) * W, :], ta_lo[k * W : (k + 1) * W, :] = table(pa, k, W)
    loads[1].wait()
    for k in range(K):
        tb_hi[k * R : (k + 1) * R, :], tb_lo[k * R : (k + 1) * R, :] = table(pb, k, R)

    loads[2].wait()
    loads[3].wait()
    m = mask[...].astype(f32)
    for k in range(K):
        hi, lo = split(basis[k] * m)
        src_r[0:R, k * W : (k + 1) * W] = hi
        src_r[R : 2 * R, k * W : (k + 1) * W] = lo
        src_c[k * R : (k + 1) * R, 0:W] = hi
        src_c[k * R : (k + 1) * R, W : 2 * W] = lo

    part = dot(src_r[...], ta_hi[...], 1, 0) + dot(src_r[...], ta_lo[...], 1, 0)
    part = part[:R] + part[R:]
    for level in range(CL):
        cp[level] = part[:, level * W : (level + 1) * W]
    pl.semaphore_wait(barrier, len(peers))
    s_c1 = [copy(cp.at[d], c1.at[d], along_y(d)) for d in (2, 1, 3)]
    for s in s_c1:
        s.start()

    part = dot(tb_hi[...], src_c[...], 0, 0) + dot(tb_lo[...], src_c[...], 0, 0)
    part = part[:, :W] + part[:, W:]
    for level in range(9):
        block = part[level * R : (level + 1) * R]
        if level % 2:
            odd[level // 2] = block
        else:
            even[level // 2] = block
    s_r1 = copy(odd, r1, core())
    s_r1.start()
    for s in loads[4:]:
        s.wait()
    alpha = scal[0]
    base = 1.0 / (1.0 + 0.25 * wcode[...].astype(f32))
    weight_a = jnp.where(rcode[...] != 2, base, 0.0)
    weight_b = jnp.where(rcode[...] != 1, base, 0.0)

    s_r1.wait_recv()
    for i in range(4):
        even[1 - c + i] = even[1 - c + i] + r1[i]
    s_r2 = [copy(even.at[d], r2.at[d], run(d)) for d in (1, 2, 3)]
    for s in s_r2:
        s.start()

    for s in s_c1:
        s.wait_recv()
    here, there = cp[0], cp[4]
    for d in (1, 2, 3):
        mine = d <= y
        here = here + jnp.where(mine, c1[d], 0.0)
        there = there + jnp.where(mine, 0.0, c1[d])
    cp[4] = there
    s_c2 = copy(cp.at[4], c2, far(1))
    s_c2.start()

    for s in s_r2:
        s.wait_recv()
    rows_here, there = even[0], even[4]
    for d in (1, 2, 3):
        mine = d <= z
        rows_here = rows_here + jnp.where(mine, r2[d], 0.0)
        there = there + jnp.where(mine, 0.0, r2[d])
    even[4] = there
    s_r3 = copy(even.at[4], r3, along_x(1))
    s_r3.start()

    s_c2.wait_recv()
    image = here + jnp.where(h > 0, c2[...], 0.0)
    ra = weight_a * image - alpha * resid_a[...]
    raw_a[...] = ra
    wa = weight_a * ra
    ext_c[0] = wa
    s_d1 = copy(ext_c.at[0], ext_c.at[4], far(3))
    s_d1.start()
    s_d2 = []
    for d in (1, 2, 3):
        to = along_y(d)
        s = copy(ext_c.at[0], ext_c.at[4 - d], to)
        later = copy(ext_c.at[4], ext_c.at[4 - d], to, again=True)
        s_d2.append((s, later, y + d >= 4))
    for s, later, now in s_d2:
        pl.when(now)(s.start)

    s_r3.wait_recv()
    image = rows_here + jnp.where(x > 0, r3[...], 0.0)
    rb = weight_b * image - alpha * resid_b[...]
    raw_b[...] = rb
    wb = weight_b * rb
    ext_e[0] = wb
    s_a1 = copy(ext_e.at[0], ext_e.at[4], along_x(3))
    s_a1.start()
    s_a2 = []
    for d in (1, 2, 3):
        to = run(d)
        s = copy(ext_e.at[0], ext_e.at[4 - d], to)
        later = copy(ext_e.at[4], ext_e.at[4 - d], to, again=True)
        s_a2.append((s, later, z + d >= 4))
    for s, later, now in s_a2:
        pl.when(now)(s.start)

    def tile_of(q):
        t = jnp.sum(q.reshape(-1, 8, W), axis=0)
        t = t + pltpu.roll(t, 64, 1)
        return t + pltpu.roll(t, 32, 1)

    rr = tile_of(ra * ra + rb * rb)
    sq = jnp.zeros((R, W), f32)
    for k in range(K):
        sq = sq + basis[k] * basis[k]
    vv = tile_of(sq)

    s_d1.wait_recv()
    ext_c[4] = jnp.where(h < 3, ext_c[4], 0.0)
    for s, later, now in s_d2:
        pl.when(jnp.logical_not(now))(later.start)
    s_a1.wait_recv()
    ext_e[4] = jnp.where(x < 3, ext_e[4], 0.0)
    for s, later, now in s_a2:
        pl.when(jnp.logical_not(now))(later.start)

    def put_a(level, block):
        hi, lo = split(block)
        wext_a[0:R, level * W : (level + 1) * W] = hi
        wext_a[R : 2 * R, level * W : (level + 1) * W] = lo

    def put_b(level, block):
        hi, lo = split(block)
        wext_b[level * R : (level + 1) * R, 0:W] = hi
        wext_b[level * R : (level + 1) * R, W : 2 * W] = lo

    put_a(0, wa)
    put_a(4, ext_c[4])
    put_b(0, wb)
    put_b(8, ext_e[4])
    put_b(9, jnp.zeros((R, W), f32))

    for s, _, _ in s_a2:
        s.wait_recv()
    s_a3 = copy(ext_e.at[pl.ds(1 - c, 4)], ext_o, core())
    s_a3.start()
    for d in (1, 2, 3):
        put_b(2 * d, ext_e[d])
    for s, _, _ in s_d2:
        s.wait_recv()
    for d in (1, 2, 3):
        put_a(d, ext_c[d])
    ga = dot(wext_a[...], ta_hi[...], 1, 1) + dot(wext_a[...], ta_lo[...], 1, 1)
    ga = ga[:R] + ga[R:]
    for k in range(K):
        raw_v[k] = ga[:, k * W : (k + 1) * W]
    s_a3.wait_recv()
    for d in range(4):
        put_b(2 * d + 1, ext_o[d])
    gb = dot(tb_hi[...], wext_b[...], 1, 0) + dot(tb_lo[...], wext_b[...], 1, 0)
    gb = gb[:, :W] + gb[:, W:]
    zz = jnp.zeros((R, W), f32)
    zv = jnp.zeros((R, W), f32)
    for k in range(K):
        g = m * (raw_v[k] + gb[k * R : (k + 1) * R])
        raw_v[k] = g
        zz = zz + g * g
        zv = zv + g * basis[k]

    stores = [(raw_v, raw_v_h), (raw_a, raw_a_h), (raw_b, raw_b_h), (coef, coef_h)]
    stores = [pltpu.make_async_copy(a, b, load_sem.at[i]) for i, (a, b) in enumerate(stores)]

    quarter = lax.broadcasted_iota(jnp.int32, (8, W), 1) // (W // 4)
    both = jnp.where(quarter == 0, rr, vv)
    tile = jnp.where(quarter == 2, tile_of(zz), jnp.where(quarter == 3, tile_of(zv), both))
    sums_plane[0:1, :] = jnp.sum(tile, axis=0, keepdims=True)
    group = [copy(sums_plane.at[pl.ds(0, 1)], sums_plane.at[pl.ds(i + 1, 1)], plane(o)) for i, o in enumerate(PLANE)]
    for s in group:
        s.start()
    for s in group:
        s.wait_recv()
    sums_line[0:1, :] = jnp.sum(sums_plane[...], axis=0, keepdims=True)
    group = [copy(sums_line.at[pl.ds(0, 1)], sums_line.at[pl.ds(i + 1, 1)], line(d)) for i, d in enumerate(LINE)]
    for s in group:
        s.start()
    for s in stores[:3]:
        s.start()
    for s in group:
        s.wait_recv()
    row = jnp.sum(sums_line[...], axis=0, keepdims=True)
    mine = quarter == lax.broadcasted_iota(jnp.int32, (8, W), 0)
    sums = jnp.sum(jnp.where(mine, row, 0.0), axis=1, keepdims=True)
    beta_square = sums[0:1] + EPS
    beta = jnp.sqrt(beta_square)
    inv_beta = 1.0 / beta
    alpha_next = jnp.sqrt(sums[2:3] / beta_square - 2.0 * sums[3:4] + beta_square * sums[1:2] + EPS)
    inv_alpha = 1.0 / alpha_next
    phibar, rhobar = scal[1], scal[2]
    rho = jnp.sqrt(rhobar * rhobar + beta_square)
    cosine = rhobar / rho
    sine = beta / rho
    theta = sine * alpha_next
    phi = cosine * phibar
    values = (inv_beta, inv_beta * inv_alpha, beta * inv_alpha, phi / rho, theta / rho)
    for i, value in enumerate(values):
        coef[i : i + 1, :] = jnp.broadcast_to(value, (1, W))
    coef[5:8, :] = jnp.zeros((3, W), f32)
    stores[3].start()
    for s in started:
        s.wait_send()
    for s in stores:
        s.wait()


N_COPIES = 18 + len(PLANE) + len(LINE)


def finish(
    grad_h, raw_a_h, raw_b_h, coef_h, sol_h, search_h, basis_h,
    sol_o, search_o, basis_o, resid_a_o, resid_b_o,
    grad, raw_a, raw_b, coef, sol, search, basis, load_sem, store_sem,
):
    pairs = (
        (coef_h, coef), (search_h, search), (sol_h, sol), (grad_h, grad), (basis_h, basis), (raw_a_h, raw_a), (raw_b_h, raw_b),
    )
    loads = [pltpu.make_async_copy(a, b, load_sem.at[i]) for i, (a, b) in enumerate(pairs)]
    for s in loads:
        s.start()
    pairs = ((sol, sol_o), (grad, basis_o), (search, search_o), (raw_a, resid_a_o), (raw_b, resid_b_o))
    stores = [pltpu.make_async_copy(a, b, store_sem.at[i]) for i, (a, b) in enumerate(pairs)]
    for s in loads[:3]:
        s.wait()
    inv_beta, scale, shift = coef[0:1, :], coef[1:2, :], coef[2:3, :]
    step, turn = coef[3:4, :], coef[4:5, :]
    sol[...] = sol[...] + step * search[...]
    stores[0].start()
    for s in loads[3:5]:
        s.wait()
    v = grad[...] * scale - shift * basis[...]
    grad[...] = v
    stores[1].start()
    search[...] = v - turn * search[...]
    stores[2].start()
    for s in loads[5:]:
        s.wait()
    raw_a[...] = raw_a[...] * inv_beta
    stores[3].start()
    raw_b[...] = raw_b[...] * inv_beta
    stores[4].start()
    for s in stores:
        s.wait()


def body(sol, search, basis, resid_a, resid_b, scal, pa, pb, mask, wcode, rcode):
    hbm = pl.BlockSpec(memory_space=pltpu.HBM)
    image = jax.ShapeDtypeStruct((R, W), f32)
    maps = jax.ShapeDtypeStruct((K, R, W), f32)
    words = pltpu.VMEM((R, W), jnp.int32)
    outs = pl.pallas_call(
        kernel,
        out_shape=(maps, image, image, jax.ShapeDtypeStruct((8, W), f32)),
        in_specs=[hbm] * 9,
        out_specs=(hbm,) * 4,
        scratch_shapes=[
            pltpu.VMEM((K, R, W), f32),
            pltpu.VMEM((R, W), f32),
            pltpu.VMEM((R, W), f32),
            pltpu.VMEM((8, W), f32),
            pltpu.VMEM((K, R, W), f32),
            pltpu.VMEM((R, W), f32),
            pltpu.VMEM((R, W), f32),
            pltpu.SMEM((3,), f32),
            pltpu.VMEM((K, L), f32),
            pltpu.VMEM((K, L), f32),
            words,
            words,
            words,
            pltpu.VMEM((2 * R, K * W), bf16),
            pltpu.VMEM((K * R, 2 * W), bf16),
            pltpu.VMEM((K * W, EXT), bf16),
            pltpu.VMEM((K * W, EXT), bf16),
            pltpu.VMEM((K * R, EXT), bf16),
            pltpu.VMEM((K * R, EXT), bf16),
            pltpu.VMEM((2 * R, EXT), bf16),
            pltpu.VMEM((EXT, 2 * W), bf16),
            pltpu.VMEM((5, R, W), f32),
            pltpu.VMEM((4, R, W), f32),
            pltpu.VMEM((4, R, W), f32),
            pltpu.VMEM((4, R, W), f32),
            pltpu.VMEM((R, W), f32),
            pltpu.VMEM((5, R, W), f32),
            pltpu.VMEM((4, R, W), f32),
            pltpu.VMEM((R, W), f32),
            pltpu.VMEM((5, R, W), f32),
            pltpu.VMEM((5, R, W), f32),
            pltpu.VMEM((4, R, W), f32),
            pltpu.VMEM((1 + len(PLANE), W), f32),
            pltpu.VMEM((1 + len(LINE), W), f32),
            pltpu.SemaphoreType.DMA((N_COPIES,)),
            pltpu.SemaphoreType.DMA((N_COPIES,)),
            pltpu.SemaphoreType.DMA((9,)),
        ],
        compiler_params=pltpu.CompilerParams(
            collective_id=0, has_side_effects=True, vmem_limit_bytes=56 * 1024 * 1024
        ),
    )(basis, resid_a, resid_b, scal, pa, pb, mask, wcode, rcode)
    return pl.pallas_call(
        finish,
        out_shape=(maps, maps, maps, image, image),
        in_specs=[hbm] * 7,
        out_specs=(hbm,) * 5,
        scratch_shapes=[
            pltpu.VMEM((K, R, W), f32),
            pltpu.VMEM((R, W), f32),
            pltpu.VMEM((R, W), f32),
            pltpu.VMEM((8, W), f32),
            pltpu.VMEM((K, R, W), f32),
            pltpu.VMEM((K, R, W), f32),
            pltpu.VMEM((K, R, W), f32),
            pltpu.SemaphoreType.DMA((7,)),
            pltpu.SemaphoreType.DMA((5,)),
        ],
        compiler_params=pltpu.CompilerParams(vmem_limit_bytes=56 * 1024 * 1024),
    )(*outs, sol, search, basis)


def solution(mesh):
    torus = Mesh(mesh.devices.reshape(4, 4, 2, 4, 4), (X, Z, C, H, Y))
    maps, image = P(None, ROW, COL), P(ROW, COL)
    return jax.shard_map(
        body,
        mesh=torus,
        in_specs=(maps, maps, maps, image, image, P(), P(), P(), image, image, image),
        out_specs=(maps, maps, maps, image, image),
        check_vma=False,
    )
```

```python
import jax
import jax.numpy as jnp
from jax import lax
from jax.experimental import pallas as pl
from jax.experimental.pallas import tpu as pltpu
from jax.sharding import Mesh
from jax.sharding import PartitionSpec as P

X, Z, C, H, Y = "row_0", "row_1", "row_2", "col_0", "col_1"
ROW = (X, Z, C)
COL = (H, Y)
MESH = pl.DeviceIdType.MESH
f32 = jnp.float32
bf16 = jnp.bfloat16
EPS = 1e-12

K, L, R, W = 8, 512, 64, 128
CL = 5
EXT = CL * W


def ring(a, n):
    return min(a, n - a)


PLANE = [(dx, dy, dc) for dx in range(4) for dy in range(4) for dc in range(2)][1:]
PLANE.sort(key=lambda o: -(ring(o[0], 4) + ring(o[1], 4)))
LINE = sorted(range(1, 16), key=lambda d: -ring(d, 16))


def split(x):
    hi = x.astype(bf16)
    return hi, (x - hi.astype(f32)).astype(bf16)


def dot(a, b, ca, cb):
    return lax.dot_general(a, b, (((ca,), (cb,)), ((), ())), preferred_element_type=f32)


def kernel(
    basis_h, resid_a_h, resid_b_h, scal_h, pa_h, pb_h, mask_h, wcode_h, rcode_h,
    raw_v_h, raw_a_h, raw_b_h, coef_h,
    raw_v, raw_a, raw_b, coef, basis, resid_a, resid_b, scal, pa, pb, mask, wcode, rcode,
    src_r, src_c, ta_hi, ta_lo, tb_hi, tb_lo, wext_a, wext_b,
    even, odd, r1, r2, r3, cp, c1, c2, ext_c, ext_e, ext_o,
    sums_plane, sums_line, send_sem, recv_sem, sum_sem, load_sem,
):
    x, z, c, h, y = (lax.axis_index(a) for a in (X, Z, C, H, Y))
    started = []

    def core():
        return {C: 1 - c}

    def run(d):
        return {Z: lax.rem(z + d, 4)}

    def along_x(d):
        return {X: lax.rem(x + d, 4)}

    def along_y(d):
        return {Y: lax.rem(y + d, 4)}

    def far(d):
        return {H: lax.rem(h + d, 4)}

    def plane(o):
        return {X: lax.rem(x + o[0], 4), Y: lax.rem(y + o[1], 4), C: lax.rem(c + o[2], 2)}

    def line(d):
        at = 4 * h + z + d
        return {H: lax.rem(at // 4, 4), Z: lax.rem(at, 4)}

    def copy(src, dst, to, again=False):
        i = len(started) - again
        d = pltpu.make_async_remote_copy(
            src_ref=src, dst_ref=dst, send_sem=send_sem.at[i], recv_sem=recv_sem.at[i], device_id=to, device_id_type=MESH
        )
        if not again:
            started.append(d)
        return d

    def share(sums, offsets, to, n):
        rows = sums.at[pl.ds(0, 1)]
        for i, o in enumerate(offsets):
            pltpu.make_async_remote_copy(
                src_ref=rows, dst_ref=sums.at[pl.ds(i + 1, 1)], send_sem=sum_sem.at[n], recv_sem=sum_sem.at[n + 1],
                device_id=to(o), device_id_type=MESH,
            ).start()
        others = sums.at[pl.ds(1, len(offsets))]
        return pltpu.make_async_remote_copy(
            src_ref=others, dst_ref=others, send_sem=sum_sem.at[n], recv_sem=sum_sem.at[n + 1],
            device_id=to(offsets[0]), device_id_type=MESH,
        )

    barrier = pltpu.get_barrier_semaphore()
    peers = [core()] + [run(d) for d in (1, 2, 3)] + [along_y(d) for d in (1, 2, 3)]
    peers += [along_x(1), along_x(3), far(1), far(3)]
    for to in peers:
        pl.semaphore_signal(barrier, inc=1, device_id=to, device_id_type=MESH)

    pairs = (
        (pa_h, pa), (pb_h, pb), (mask_h, mask), (basis_h, basis), (scal_h, scal), (wcode_h, wcode),
        (rcode_h, rcode), (resid_a_h, resid_a), (resid_b_h, resid_b),
    )
    loads = [pltpu.make_async_copy(a, b, load_sem.at[i]) for i, (a, b) in enumerate(pairs)]
    for s in loads:
        s.start()

    pad = jnp.zeros((1, EXT - L), f32)

    def table(profile, k, rows):
        row = jnp.concatenate([profile[k : k + 1, :], pad], axis=1)
        return split(pltpu.roll(jnp.broadcast_to(row, (rows, EXT)), 0, 1, stride=1, stride_axis=0))

    loads[0].wait()
    for k in range(K):
        ta_hi[k * W : (k + 1) * W, :], ta_lo[k * W : (k + 1) * W, :] = table(pa, k, W)

    loads[2].wait()
    loads[3].wait()
    m = mask[...].astype(f32)
    for k in range(K):
        hi, lo = split(basis[k] * m)
        src_r[0:R, k * W : (k + 1) * W] = hi
        src_r[R : 2 * R, k * W : (k + 1) * W] = lo
        src_c[k * R : (k + 1) * R, 0:W] = hi
        src_c[k * R : (k + 1) * R, W : 2 * W] = lo

    part = dot(src_r[...], ta_hi[...], 1, 0) + dot(src_r[...], ta_lo[...], 1, 0)
    part = part[:R] + part[R:]
    for level in range(CL):
        cp[level] = part[:, level * W : (level + 1) * W]
    pl.semaphore_wait(barrier, len(peers))
    s_c1 = [copy(cp.at[d], c1.at[d], along_y(d)) for d in (2, 1, 3)]
    for s in s_c1:
        s.start()

    loads[1].wait()
    for k in range(K):
        tb_hi[k * R : (k + 1) * R, :], tb_lo[k * R : (k + 1) * R, :] = table(pb, k, R)

    part = dot(tb_hi[...], src_c[...], 0, 0) + dot(tb_lo[...], src_c[...], 0, 0)
    part = part[:, :W] + part[:, W:]
    for level in range(9):
        block = part[level * R : (level + 1) * R]
        if level % 2:
            odd[level // 2] = block
        else:
            even[level // 2] = block
    s_r1 = copy(odd, r1, core())
    s_r1.start()
    for s in loads[4:]:
        s.wait()
    alpha = scal[0]
    base = 1.0 / (1.0 + 0.25 * wcode[...].astype(f32))
    weight_a = jnp.where(rcode[...] != 2, base, 0.0)
    weight_b = jnp.where(rcode[...] != 1, base, 0.0)

    s_r1.wait_recv()
    for i in range(4):
        even[1 - c + i] = even[1 - c + i] + r1[i]
    s_r2 = [copy(even.at[d], r2.at[d], run(d)) for d in (1, 2, 3)]
    for s in s_r2:
        s.start()

    for s in s_c1:
        s.wait_recv()
    here, there = cp[0], cp[4]
    for d in (1, 2, 3):
        mine = d <= y
        here = here + jnp.where(mine, c1[d], 0.0)
        there = there + jnp.where(mine, 0.0, c1[d])
    cp[4] = there
    s_c2 = copy(cp.at[4], c2, far(1))
    pl.when(h < 3)(s_c2.start)

    for s in s_r2:
        s.wait_recv()
    rows_here, there = even[0], even[4]
    for d in (1, 2, 3):
        mine = d <= z
        rows_here = rows_here + jnp.where(mine, r2[d], 0.0)
        there = there + jnp.where(mine, 0.0, r2[d])
    even[4] = there
    s_r3 = copy(even.at[4], r3, along_x(1))
    pl.when(x < 3)(s_r3.start)

    pl.when(h > 0)(s_c2.wait_recv)
    image = here + jnp.where(h > 0, c2[...], 0.0)
    ra = weight_a * image - alpha * resid_a[...]
    raw_a[...] = ra
    wa = weight_a * ra
    ext_c[0] = wa
    s_d1 = copy(ext_c.at[0], ext_c.at[4], far(3))
    pl.when(h > 0)(s_d1.start)
    s_d2 = []
    for d in (1, 2, 3):
        to = along_y(d)
        s = copy(ext_c.at[0], ext_c.at[4 - d], to)
        later = copy(ext_c.at[4], ext_c.at[4 - d], to, again=True)
        s_d2.append((s, later, y + d >= 4))
    for s, later, now in s_d2:
        pl.when(now)(s.start)

    pl.when(x > 0)(s_r3.wait_recv)
    image = rows_here + jnp.where(x > 0, r3[...], 0.0)
    rb = weight_b * image - alpha * resid_b[...]
    raw_b[...] = rb
    wb = weight_b * rb
    ext_e[0] = wb
    s_a1 = copy(ext_e.at[0], ext_e.at[4], along_x(3))
    pl.when(x > 0)(s_a1.start)
    s_a2 = []
    for d in (1, 2, 3):
        to = run(d)
        s = copy(ext_e.at[0], ext_e.at[4 - d], to)
        later = copy(ext_e.at[4], ext_e.at[4 - d], to, again=True)
        s_a2.append((s, later, z + d >= 4))
    for s, later, now in s_a2:
        pl.when(now)(s.start)

    def tile_of(q):
        t = jnp.sum(q.reshape(-1, 8, W), axis=0)
        t = t + pltpu.roll(t, 64, 1)
        return t + pltpu.roll(t, 32, 1)

    rr = tile_of(ra * ra + rb * rb)
    sq = jnp.zeros((R, W), f32)
    for k in range(K):
        sq = sq + basis[k] * basis[k]
    vv = tile_of(sq)

    pl.when(x < 3)(s_a1.wait_recv)
    ext_e[4] = jnp.where(x < 3, ext_e[4], 0.0)
    for s, later, now in s_a2:
        pl.when(jnp.logical_not(now))(later.start)
    pl.when(h < 3)(s_d1.wait_recv)
    ext_c[4] = jnp.where(h < 3, ext_c[4], 0.0)
    for s, later, now in s_d2:
        pl.when(jnp.logical_not(now))(later.start)

    def put_a(level, block):
        hi, lo = split(block)
        wext_a[0:R, level * W : (level + 1) * W] = hi
        wext_a[R : 2 * R, level * W : (level + 1) * W] = lo

    def put_b(level, block):
        hi, lo = split(block)
        wext_b[level * R : (level + 1) * R, 0:W] = hi
        wext_b[level * R : (level + 1) * R, W : 2 * W] = lo

    put_a(0, wa)
    put_a(4, ext_c[4])
    put_b(0, wb)
    put_b(8, ext_e[4])
    put_b(9, jnp.zeros((R, W), f32))

    ends = wext_a[:, :W], wext_a[:, EXT - W :]
    tables = ta_hi, ta_lo
    ga = sum(dot(w, t[:, at], 1, 1) for t in tables for w, at in zip(ends, (slice(0, W), slice(EXT - W, EXT))))
    ga = ga[:R] + ga[R:]
    for k in range(K):
        raw_v[k] = ga[:, k * W : (k + 1) * W]
    for s, _, _ in s_a2:
        s.wait_recv()
    s_a3 = copy(ext_e.at[pl.ds(1 - c, 4)], ext_o, core())
    s_a3.start()
    for d in (1, 2, 3):
        put_b(2 * d, ext_e[d])
    s_a3.wait_recv()
    for d in range(4):
        put_b(2 * d + 1, ext_o[d])
    gb = dot(tb_hi[...], wext_b[...], 1, 0) + dot(tb_lo[...], wext_b[...], 1, 0)
    gb = gb[:, :W] + gb[:, W:]
    for k in range(K):
        raw_v[k] = raw_v[k] + gb[k * R : (k + 1) * R]
    for s, _, _ in s_d2:
        s.wait_recv()
    for d in (1, 2, 3):
        put_a(d, ext_c[d])
    middle = slice(W, EXT - W)
    ga = dot(wext_a[:, middle], ta_hi[:, middle], 1, 1) + dot(wext_a[:, middle], ta_lo[:, middle], 1, 1)
    ga = ga[:R] + ga[R:]
    zz = jnp.zeros((R, W), f32)
    zv = jnp.zeros((R, W), f32)
    for k in range(K):
        g = m * (raw_v[k] + ga[:, k * W : (k + 1) * W])
        raw_v[k] = g
        zz = zz + g * g
        zv = zv + g * basis[k]

    stores = [(raw_v, raw_v_h), (raw_a, raw_a_h), (raw_b, raw_b_h), (coef, coef_h)]
    stores = [pltpu.make_async_copy(a, b, load_sem.at[i]) for i, (a, b) in enumerate(stores)]

    quarter = lax.broadcasted_iota(jnp.int32, (8, W), 1) // (W // 4)
    both = jnp.where(quarter == 0, rr, vv)
    tile = jnp.where(quarter == 2, tile_of(zz), jnp.where(quarter == 3, tile_of(zv), both))
    sums_plane[0:1, :] = jnp.sum(tile, axis=0, keepdims=True)
    group_plane = share(sums_plane, PLANE, plane, 0)
    for s in stores[:3]:
        s.start()
    sent = {id(s_c2): h < 3, id(s_r3): x < 3, id(s_d1): h > 0, id(s_a1): x > 0}
    for s in started:
        pl.when(sent.get(id(s), True))(s.wait_send)
    group_plane.wait_recv()
    sums_line[0:1, :] = jnp.sum(sums_plane[...], axis=0, keepdims=True)
    group_line = share(sums_line, LINE, line, 2)
    group_plane.wait_send()
    for s in stores[:3]:
        s.wait()
    group_line.wait_recv()
    row = jnp.sum(sums_line[...], axis=0, keepdims=True)
    mine = quarter == lax.broadcasted_iota(jnp.int32, (8, W), 0)
    sums = jnp.sum(jnp.where(mine, row, 0.0), axis=1, keepdims=True)
    beta_square = sums[0:1] + EPS
    beta = jnp.sqrt(beta_square)
    inv_beta = 1.0 / beta
    alpha_next = jnp.sqrt(sums[2:3] / beta_square - 2.0 * sums[3:4] + beta_square * sums[1:2] + EPS)
    inv_alpha = 1.0 / alpha_next
    phibar, rhobar = scal[1], scal[2]
    rho = jnp.sqrt(rhobar * rhobar + beta_square)
    cosine = rhobar / rho
    sine = beta / rho
    theta = sine * alpha_next
    phi = cosine * phibar
    values = (inv_beta, inv_beta * inv_alpha, beta * inv_alpha, phi / rho, theta / rho)
    for i, value in enumerate(values):
        coef[i : i + 1, :] = jnp.broadcast_to(value, (1, W))
    coef[5:8, :] = jnp.zeros((3, W), f32)
    stores[3].start()
    group_line.wait_send()
    stores[3].wait()


N_COPIES = 18


def finish(
    grad_h, raw_a_h, raw_b_h, coef_h, sol_h, search_h, basis_h,
    sol_o, search_o, basis_o, resid_a_o, resid_b_o,
    grad, raw_a, raw_b, coef, sol, search, basis, load_sem, store_sem,
):
    pairs = (
        (coef_h, coef), (search_h, search), (sol_h, sol), (grad_h, grad), (basis_h, basis), (raw_a_h, raw_a), (raw_b_h, raw_b),
    )
    loads = [pltpu.make_async_copy(a, b, load_sem.at[i]) for i, (a, b) in enumerate(pairs)]
    for s in loads:
        s.start()
    pairs = ((sol, sol_o), (grad, basis_o), (search, search_o), (raw_a, resid_a_o), (raw_b, resid_b_o))
    stores = [pltpu.make_async_copy(a, b, store_sem.at[i]) for i, (a, b) in enumerate(pairs)]
    for s in loads[:3]:
        s.wait()
    inv_beta, scale, shift = coef[0:1, :], coef[1:2, :], coef[2:3, :]
    step, turn = coef[3:4, :], coef[4:5, :]
    sol[...] = sol[...] + step * search[...]
    stores[0].start()
    for s in loads[3:5]:
        s.wait()
    v = grad[...] * scale - shift * basis[...]
    grad[...] = v
    stores[1].start()
    search[...] = v - turn * search[...]
    stores[2].start()
    for s in loads[5:]:
        s.wait()
    raw_a[...] = raw_a[...] * inv_beta
    stores[3].start()
    raw_b[...] = raw_b[...] * inv_beta
    stores[4].start()
    for s in stores:
        s.wait()


def body(sol, search, basis, resid_a, resid_b, scal, pa, pb, mask, wcode, rcode):
    hbm = pl.BlockSpec(memory_space=pltpu.HBM)
    image = jax.ShapeDtypeStruct((R, W), f32)
    maps = jax.ShapeDtypeStruct((K, R, W), f32)
    words = pltpu.VMEM((R, W), jnp.int32)
    outs = pl.pallas_call(
        kernel,
        out_shape=(maps, image, image, jax.ShapeDtypeStruct((8, W), f32)),
        in_specs=[hbm] * 9,
        out_specs=(hbm,) * 4,
        scratch_shapes=[
            pltpu.VMEM((K, R, W), f32),
            pltpu.VMEM((R, W), f32),
            pltpu.VMEM((R, W), f32),
            pltpu.VMEM((8, W), f32),
            pltpu.VMEM((K, R, W), f32),
            pltpu.VMEM((R, W), f32),
            pltpu.VMEM((R, W), f32),
            pltpu.SMEM((3,), f32),
            pltpu.VMEM((K, L), f32),
            pltpu.VMEM((K, L), f32),
            words,
            words,
            words,
            pltpu.VMEM((2 * R, K * W), bf16),
            pltpu.VMEM((K * R, 2 * W), bf16),
            pltpu.VMEM((K * W, EXT), bf16),
            pltpu.VMEM((K * W, EXT), bf16),
            pltpu.VMEM((K * R, EXT), bf16),
            pltpu.VMEM((K * R, EXT), bf16),
            pltpu.VMEM((2 * R, EXT), bf16),
            pltpu.VMEM((EXT, 2 * W), bf16),
            pltpu.VMEM((5, R, W), f32),
            pltpu.VMEM((4, R, W), f32),
            pltpu.VMEM((4, R, W), f32),
            pltpu.VMEM((4, R, W), f32),
            pltpu.VMEM((R, W), f32),
            pltpu.VMEM((5, R, W), f32),
            pltpu.VMEM((4, R, W), f32),
            pltpu.VMEM((R, W), f32),
            pltpu.VMEM((5, R, W), f32),
            pltpu.VMEM((5, R, W), f32),
            pltpu.VMEM((4, R, W), f32),
            pltpu.VMEM((1 + len(PLANE), W), f32),
            pltpu.VMEM((1 + len(LINE), W), f32),
            pltpu.SemaphoreType.DMA((N_COPIES,)),
            pltpu.SemaphoreType.DMA((N_COPIES,)),
            pltpu.SemaphoreType.DMA((4,)),
            pltpu.SemaphoreType.DMA((9,)),
        ],
        compiler_params=pltpu.CompilerParams(
            collective_id=0, has_side_effects=True, vmem_limit_bytes=56 * 1024 * 1024
        ),
    )(basis, resid_a, resid_b, scal, pa, pb, mask, wcode, rcode)
    return pl.pallas_call(
        finish,
        out_shape=(maps, maps, maps, image, image),
        in_specs=[hbm] * 7,
        out_specs=(hbm,) * 5,
        scratch_shapes=[
            pltpu.VMEM((K, R, W), f32),
            pltpu.VMEM((R, W), f32),
            pltpu.VMEM((R, W), f32),
            pltpu.VMEM((8, W), f32),
            pltpu.VMEM((K, R, W), f32),
            pltpu.VMEM((K, R, W), f32),
            pltpu.VMEM((K, R, W), f32),
            pltpu.SemaphoreType.DMA((7,)),
            pltpu.SemaphoreType.DMA((5,)),
        ],
        compiler_params=pltpu.CompilerParams(vmem_limit_bytes=56 * 1024 * 1024),
    )(*outs, sol, search, basis)


def solution(mesh):
    torus = Mesh(mesh.devices.reshape(4, 4, 2, 4, 4), (X, Z, C, H, Y))
    maps, image = P(None, ROW, COL), P(ROW, COL)
    return jax.shard_map(
        body,
        mesh=torus,
        in_specs=(maps, maps, maps, image, image, P(), P(), P(), image, image, image),
        out_specs=(maps, maps, maps, image, image),
        check_vma=False,
    )
```

```python
import jax
import jax.numpy as jnp
from jax import lax
from jax.experimental import pallas as pl
from jax.experimental.pallas import tpu as pltpu
from jax.sharding import Mesh
from jax.sharding import PartitionSpec as P

X, Z, C, H, Y = "row_0", "row_1", "row_2", "col_0", "col_1"
ROW = (X, Z, C)
COL = (H, Y)
MESH = pl.DeviceIdType.MESH
f32 = jnp.float32
bf16 = jnp.bfloat16
EPS = 1e-12

K, L, R, W = 8, 512, 64, 128
CL = 5
EXT = CL * W


def ring(a, n):
    return min(a, n - a)


PLANE = [(dx, dy, dc) for dx in range(4) for dy in range(4) for dc in range(2)][1:]
PLANE.sort(key=lambda o: -(ring(o[0], 4) + ring(o[1], 4)))
LINE = sorted(range(1, 16), key=lambda d: -ring(d, 16))


def split(x):
    hi = x.astype(bf16)
    return hi, (x - hi.astype(f32)).astype(bf16)


def dot(a, b, ca, cb):
    return lax.dot_general(a, b, (((ca,), (cb,)), ((), ())), preferred_element_type=f32)


def kernel(
    basis_h, resid_a_h, resid_b_h, scal_h, pa_h, pb_h, mask_h, wcode_h, rcode_h,
    raw_v_h, raw_a_h, raw_b_h, coef_h,
    raw_v, raw_a, raw_b, coef, basis, resid_a, resid_b, scal, pa, pb, mask, wcode, rcode,
    src_r, src_c, ta_hi, ta_lo, tb_hi, tb_lo, wext_a, wext_b,
    even, odd, r1, r2, r3, cp, c1, c2, ext_c, ext_e, ext_o,
    sums_plane, sums_line, send_sem, recv_sem, sum_sem, load_sem, ready,
    square_a, square_b, next_square_a, next_square_b, next_a, next_b,
):
    x, z, c, h, y = (lax.axis_index(a) for a in (X, Z, C, H, Y))
    started = []

    def core():
        return {C: 1 - c}

    def run(d):
        return {Z: lax.rem(z + d, 4)}

    def along_x(d):
        return {X: lax.rem(x + d, 4)}

    def along_y(d):
        return {Y: lax.rem(y + d, 4)}

    def far(d):
        return {H: lax.rem(h + d, 4)}

    def plane(o):
        return {X: lax.rem(x + o[0], 4), Y: lax.rem(y + o[1], 4), C: lax.rem(c + o[2], 2)}

    def line(d):
        at = 4 * h + z + d
        return {H: lax.rem(at // 4, 4), Z: lax.rem(at, 4)}

    def copy(src, dst, to, again=False):
        i = len(started) - again
        d = pltpu.make_async_remote_copy(
            src_ref=src, dst_ref=dst, send_sem=send_sem.at[i], recv_sem=recv_sem.at[i], device_id=to, device_id_type=MESH
        )
        if not again:
            started.append(d)
        return d

    def share(sums, offsets, to, n):
        rows = sums.at[pl.ds(0, 1)]
        for i, o in enumerate(offsets):
            pltpu.make_async_remote_copy(
                src_ref=rows, dst_ref=sums.at[pl.ds(i + 1, 1)], send_sem=sum_sem.at[n], recv_sem=sum_sem.at[n + 1],
                device_id=to(o), device_id_type=MESH,
            ).start()
        others = sums.at[pl.ds(1, len(offsets))]
        return pltpu.make_async_remote_copy(
            src_ref=others, dst_ref=others, send_sem=sum_sem.at[n], recv_sem=sum_sem.at[n + 1],
            device_id=to(offsets[0]), device_id_type=MESH,
        )

    barrier = pltpu.get_barrier_semaphore()
    peers = [core()] + [run(d) for d in (1, 2, 3)] + [along_y(d) for d in (1, 2, 3)]
    peers += [along_x(1), along_x(3), far(1), far(3)]
    for to in peers:
        pl.semaphore_signal(barrier, inc=1, device_id=to, device_id_type=MESH)

    pairs = (
        (pa_h, pa), (pb_h, pb), (mask_h, mask), (basis_h, basis), (scal_h, scal), (wcode_h, wcode),
        (rcode_h, rcode), (resid_a_h, resid_a), (resid_b_h, resid_b),
    )
    loads = [pltpu.make_async_copy(a, b, load_sem.at[i]) for i, (a, b) in enumerate(pairs)]
    for s in loads:
        s.start()

    pad = jnp.zeros((1, EXT - L), f32)

    def table(profile, k, rows):
        row = jnp.concatenate([profile[k : k + 1, :], pad], axis=1)
        return split(pltpu.roll(jnp.broadcast_to(row, (rows, EXT)), 0, 1, stride=1, stride_axis=0))

    loads[0].wait()
    for k in range(K):
        ta_hi[k * W : (k + 1) * W, :], ta_lo[k * W : (k + 1) * W, :] = table(pa, k, W)

    loads[2].wait()
    loads[3].wait()
    m = mask[...].astype(f32)
    for k in range(K):
        hi, lo = split(basis[k] * m)
        src_r[0:R, k * W : (k + 1) * W] = hi
        src_r[R : 2 * R, k * W : (k + 1) * W] = lo
        src_c[k * R : (k + 1) * R, 0:W] = hi
        src_c[k * R : (k + 1) * R, W : 2 * W] = lo

    middle = slice(W, EXT - W)
    part = dot(src_r[...], ta_hi[:, middle], 1, 0) + dot(src_r[...], ta_lo[:, middle], 1, 0)
    part = part[:R] + part[R:]
    for level in (1, 2, 3):
        cp[level] = part[:, (level - 1) * W : level * W]
    for level in (0, 4):
        at = slice(level * W, (level + 1) * W)
        part = dot(src_r[...], ta_hi[:, at], 1, 0) + dot(src_r[...], ta_lo[:, at], 1, 0)
        cp[level] = part[:R] + part[R:]
    for s in loads[4:]:
        s.wait()
    alpha = scal[0]
    base = 1.0 / (1.0 + 0.25 * wcode[...].astype(f32))
    weight_a = jnp.where(rcode[...] != 2, base, 0.0)
    weight_b = jnp.where(rcode[...] != 1, base, 0.0)
    loads[1].wait()
    for k in range(K):
        tb_hi[k * R : (k + 1) * R, :], tb_lo[k * R : (k + 1) * R, :] = table(pb, k, R)

    part = dot(tb_hi[...], src_c[...], 0, 0) + dot(tb_lo[...], src_c[...], 0, 0)
    part = part[:, :W] + part[:, W:]
    for level in range(9):
        block = part[level * R : (level + 1) * R]
        if level % 2:
            odd[level // 2] = block
        else:
            even[level // 2] = block
    square_a[...] = weight_a * weight_a
    square_b[...] = weight_b * weight_b

    pl.semaphore_wait(barrier, len(peers))
    s_r1 = copy(odd, r1, core())
    s_r1.start()
    s_c1 = [copy(cp.at[d], c1.at[d], along_y(d)) for d in (2, 1, 3)]
    for s in s_c1:
        s.start()
    s_k1 = copy(square_a, next_square_a, far(3))
    pl.when(h > 0)(s_k1.start)
    s_k2 = copy(square_b, next_square_b, along_x(3))
    pl.when(x > 0)(s_k2.start)

    s_r1.wait_recv()
    for i in range(4):
        even[1 - c + i] = even[1 - c + i] + r1[i]
    s_r2 = [copy(even.at[d], r2.at[d], run(d)) for d in (1, 2, 3)]
    for s in s_r2:
        s.start()

    for s in s_c1:
        s.wait_recv()
    here, there = cp[0], cp[4]
    for d in (1, 2, 3):
        mine = d <= y
        here = here + jnp.where(mine, c1[d], 0.0)
        there = there + jnp.where(mine, 0.0, c1[d])
    beyond = there
    cp[4] = there
    s_c2 = copy(cp.at[4], c2, far(1))
    pl.when(h < 3)(s_c2.start)
    part_a = weight_a * (weight_a * here - alpha * resid_a[...])
    cp[0] = part_a
    s_d1 = copy(cp.at[0], next_a, far(3))
    pl.when(h > 0)(s_d1.start)

    for s in s_r2:
        s.wait_recv()
    rows_here, there = even[0], even[4]
    for d in (1, 2, 3):
        mine = d <= z
        rows_here = rows_here + jnp.where(mine, r2[d], 0.0)
        there = there + jnp.where(mine, 0.0, r2[d])
    even[4] = there
    s_r3 = copy(even.at[4], r3, along_x(1))
    pl.when(x < 3)(s_r3.start)
    part_b = weight_b * (weight_b * rows_here - alpha * resid_b[...])
    even[0] = part_b
    s_a1 = copy(even.at[0], next_b, along_x(3))
    pl.when(x > 0)(s_a1.start)

    pl.when(x > 0)(s_r3.wait_recv)
    came = jnp.where(x > 0, r3[...], 0.0)
    wb = part_b + square_b[...] * came
    ext_e[0] = wb
    s_a2 = []
    for d in (1, 2, 3):
        to = run(d)
        s = copy(ext_e.at[0], ext_e.at[4 - d], to)
        later = copy(ext_e.at[4], ext_e.at[4 - d], to, again=True)
        s_a2.append((s, later, z + d >= 4))
    for s, later, now in s_a2:
        pl.when(now)(s.start)
    rb = weight_b * (rows_here + came) - alpha * resid_b[...]
    raw_b[...] = rb
    pl.when(x < 3)(s_k2.wait_recv)
    pl.when(x < 3)(s_a1.wait_recv)
    ext_e[4] = jnp.where(x < 3, next_b[...] + next_square_b[...] * there, 0.0)
    for s, later, now in s_a2:
        pl.when(jnp.logical_not(now))(later.start)

    pl.when(h > 0)(s_c2.wait_recv)
    came = jnp.where(h > 0, c2[...], 0.0)
    wa = part_a + square_a[...] * came
    ext_c[0] = wa
    s_d2 = []
    for d in (1, 2, 3):
        to = along_y(d)
        s = copy(ext_c.at[0], ext_c.at[4 - d], to)
        later = copy(ext_c.at[4], ext_c.at[4 - d], to, again=True)
        s_d2.append((s, later, y + d >= 4))
    for s, later, now in s_d2:
        pl.when(now)(s.start)
    ra = weight_a * (here + came) - alpha * resid_a[...]
    raw_a[...] = ra
    pl.when(h < 3)(s_k1.wait_recv)
    pl.when(h < 3)(s_d1.wait_recv)
    ext_c[4] = jnp.where(h < 3, next_a[...] + next_square_a[...] * beyond, 0.0)
    for s, later, now in s_d2:
        pl.when(jnp.logical_not(now))(later.start)
    for d in (1, 2, 3):
        pl.semaphore_signal(ready, inc=1, device_id=run(d), device_id_type=MESH)

    def tile_of(q):
        t = jnp.sum(q.reshape(-1, 8, W), axis=0)
        t = t + pltpu.roll(t, 64, 1)
        return t + pltpu.roll(t, 32, 1)

    rr = tile_of(ra * ra + rb * rb)
    sq = jnp.zeros((R, W), f32)
    for k in range(K):
        sq = sq + basis[k] * basis[k]
    vv = tile_of(sq)

    def put_a(level, block):
        hi, lo = split(block)
        wext_a[0:R, level * W : (level + 1) * W] = hi
        wext_a[R : 2 * R, level * W : (level + 1) * W] = lo

    def put_b(level, block):
        hi, lo = split(block)
        wext_b[level * R : (level + 1) * R, 0:W] = hi
        wext_b[level * R : (level + 1) * R, W : 2 * W] = lo

    put_a(0, wa)
    put_a(4, ext_c[4])
    put_b(0, wb)
    put_b(8, ext_e[4])
    put_b(9, jnp.zeros((R, W), f32))

    ends = wext_a[:, :W], wext_a[:, EXT - W :]
    tables = ta_hi, ta_lo
    ga = sum(dot(w, t[:, at], 1, 1) for t in tables for w, at in zip(ends, (slice(0, W), slice(EXT - W, EXT))))
    ga = ga[:R] + ga[R:]
    for k in range(K):
        raw_v[k] = ga[:, k * W : (k + 1) * W]
    for s, _, _ in s_a2:
        s.wait_recv()
    s_a3 = copy(ext_e.at[pl.ds(1 - c, 4)], ext_o, core())
    s_a3.start()
    for d in (1, 2, 3):
        put_b(2 * d, ext_e[d])
    for s, _, _ in s_d2:
        s.wait_recv()
    for d in (1, 2, 3):
        put_a(d, ext_c[d])
    ga = dot(wext_a[:, middle], ta_hi[:, middle], 1, 1) + dot(wext_a[:, middle], ta_lo[:, middle], 1, 1)
    ga = ga[:R] + ga[R:]
    for k in range(K):
        raw_v[k] = raw_v[k] + ga[:, k * W : (k + 1) * W]
    s_a3.wait_recv()
    for d in range(4):
        put_b(2 * d + 1, ext_o[d])
    gb = dot(tb_hi[...], wext_b[...], 1, 0) + dot(tb_lo[...], wext_b[...], 1, 0)
    gb = gb[:, :W] + gb[:, W:]
    zz = jnp.zeros((R, W), f32)
    zv = jnp.zeros((R, W), f32)
    for k in range(K):
        g = m * (raw_v[k] + gb[k * R : (k + 1) * R])
        raw_v[k] = g
        zz = zz + g * g
        zv = zv + g * basis[k]

    stores = [(raw_v, raw_v_h), (raw_a, raw_a_h), (raw_b, raw_b_h), (coef, coef_h)]
    stores = [pltpu.make_async_copy(a, b, load_sem.at[i]) for i, (a, b) in enumerate(stores)]

    quarter = lax.broadcasted_iota(jnp.int32, (8, W), 1) // (W // 4)
    both = jnp.where(quarter == 0, rr, vv)
    tile = jnp.where(quarter == 2, tile_of(zz), jnp.where(quarter == 3, tile_of(zv), both))
    sums_plane[0:1, :] = jnp.sum(tile, axis=0, keepdims=True)
    group_plane = share(sums_plane, PLANE, plane, 0)
    for s in stores[:3]:
        s.start()
    sent = {id(s_c2): h < 3, id(s_r3): x < 3, id(s_d1): h > 0, id(s_a1): x > 0, id(s_k1): h > 0, id(s_k2): x > 0}
    for s in started:
        pl.when(sent.get(id(s), True))(s.wait_send)
    group_plane.wait_recv()
    sums_line[0:1, :] = jnp.sum(sums_plane[...], axis=0, keepdims=True)
    pl.semaphore_wait(ready, 3)
    group_line = share(sums_line, LINE, line, 2)
    group_plane.wait_send()
    for s in stores[:3]:
        s.wait()
    group_line.wait_recv()
    row = jnp.sum(sums_line[...], axis=0, keepdims=True)
    mine = quarter == lax.broadcasted_iota(jnp.int32, (8, W), 0)
    sums = jnp.sum(jnp.where(mine, row, 0.0), axis=1, keepdims=True)
    phibar, rhobar = scal[1], scal[2]
    beta_square = sums[0:1] + EPS
    inv_beta = lax.rsqrt(beta_square)
    inv_rho_square = 1.0 / (rhobar * rhobar + beta_square)
    beta = beta_square * inv_beta
    alpha_square = sums[2:3] * (inv_beta * inv_beta) - 2.0 * sums[3:4] + beta_square * sums[1:2] + EPS
    inv_alpha = lax.rsqrt(alpha_square)
    alpha_next = alpha_square * inv_alpha
    step = rhobar * phibar * inv_rho_square
    values = (inv_beta, inv_beta * inv_alpha, beta * inv_alpha, step, beta * alpha_next * inv_rho_square)
    for i, value in enumerate(values):
        coef[i : i + 1, :] = jnp.broadcast_to(value, (1, W))
    coef[5:8, :] = jnp.zeros((3, W), f32)
    stores[3].start()
    group_line.wait_send()
    stores[3].wait()


N_COPIES = 20


def finish(
    grad_h, raw_a_h, raw_b_h, coef_h, sol_h, search_h, basis_h,
    sol_o, search_o, basis_o, resid_a_o, resid_b_o,
    grad, raw_a, raw_b, coef, sol, search, basis, load_sem, store_sem,
):
    pairs = (
        (coef_h, coef), (search_h, search), (sol_h, sol), (grad_h, grad), (basis_h, basis), (raw_a_h, raw_a), (raw_b_h, raw_b),
    )
    loads = [pltpu.make_async_copy(a, b, load_sem.at[i]) for i, (a, b) in enumerate(pairs)]
    for s in loads:
        s.start()
    pairs = ((sol, sol_o), (grad, basis_o), (search, search_o), (raw_a, resid_a_o), (raw_b, resid_b_o))
    stores = [pltpu.make_async_copy(a, b, store_sem.at[i]) for i, (a, b) in enumerate(pairs)]
    for s in loads[:3]:
        s.wait()
    inv_beta, scale, shift = coef[0:1, :], coef[1:2, :], coef[2:3, :]
    step, turn = coef[3:4, :], coef[4:5, :]
    sol[...] = sol[...] + step * search[...]
    stores[0].start()
    for s in loads[3:5]:
        s.wait()
    v = grad[...] * scale - shift * basis[...]
    grad[...] = v
    stores[1].start()
    search[...] = v - turn * search[...]
    stores[2].start()
    for s in loads[5:]:
        s.wait()
    raw_a[...] = raw_a[...] * inv_beta
    stores[3].start()
    raw_b[...] = raw_b[...] * inv_beta
    stores[4].start()
    for s in stores:
        s.wait()


def body(sol, search, basis, resid_a, resid_b, scal, pa, pb, mask, wcode, rcode):
    hbm = pl.BlockSpec(memory_space=pltpu.HBM)
    image = jax.ShapeDtypeStruct((R, W), f32)
    maps = jax.ShapeDtypeStruct((K, R, W), f32)
    words = pltpu.VMEM((R, W), jnp.int32)
    outs = pl.pallas_call(
        kernel,
        out_shape=(maps, image, image, jax.ShapeDtypeStruct((8, W), f32)),
        in_specs=[hbm] * 9,
        out_specs=(hbm,) * 4,
        scratch_shapes=[
            pltpu.VMEM((K, R, W), f32),
            pltpu.VMEM((R, W), f32),
            pltpu.VMEM((R, W), f32),
            pltpu.VMEM((8, W), f32),
            pltpu.VMEM((K, R, W), f32),
            pltpu.VMEM((R, W), f32),
            pltpu.VMEM((R, W), f32),
            pltpu.SMEM((3,), f32),
            pltpu.VMEM((K, L), f32),
            pltpu.VMEM((K, L), f32),
            words,
            words,
            words,
            pltpu.VMEM((2 * R, K * W), bf16),
            pltpu.VMEM((K * R, 2 * W), bf16),
            pltpu.VMEM((K * W, EXT), bf16),
            pltpu.VMEM((K * W, EXT), bf16),
            pltpu.VMEM((K * R, EXT), bf16),
            pltpu.VMEM((K * R, EXT), bf16),
            pltpu.VMEM((2 * R, EXT), bf16),
            pltpu.VMEM((EXT, 2 * W), bf16),
            pltpu.VMEM((5, R, W), f32),
            pltpu.VMEM((4, R, W), f32),
            pltpu.VMEM((4, R, W), f32),
            pltpu.VMEM((4, R, W), f32),
            pltpu.VMEM((R, W), f32),
            pltpu.VMEM((5, R, W), f32),
            pltpu.VMEM((4, R, W), f32),
            pltpu.VMEM((R, W), f32),
            pltpu.VMEM((5, R, W), f32),
            pltpu.VMEM((5, R, W), f32),
            pltpu.VMEM((4, R, W), f32),
            pltpu.VMEM((1 + len(PLANE), W), f32),
            pltpu.VMEM((1 + len(LINE), W), f32),
            pltpu.SemaphoreType.DMA((N_COPIES,)),
            pltpu.SemaphoreType.DMA((N_COPIES,)),
            pltpu.SemaphoreType.DMA((4,)),
            pltpu.SemaphoreType.DMA((9,)),
            pltpu.SemaphoreType.REGULAR,
            *[pltpu.VMEM((R, W), f32)] * 6,
        ],
        compiler_params=pltpu.CompilerParams(
            collective_id=0, has_side_effects=True, vmem_limit_bytes=56 * 1024 * 1024
        ),
    )(basis, resid_a, resid_b, scal, pa, pb, mask, wcode, rcode)
    return pl.pallas_call(
        finish,
        out_shape=(maps, maps, maps, image, image),
        in_specs=[hbm] * 7,
        out_specs=(hbm,) * 5,
        scratch_shapes=[
            pltpu.VMEM((K, R, W), f32),
            pltpu.VMEM((R, W), f32),
            pltpu.VMEM((R, W), f32),
            pltpu.VMEM((8, W), f32),
            pltpu.VMEM((K, R, W), f32),
            pltpu.VMEM((K, R, W), f32),
            pltpu.VMEM((K, R, W), f32),
            pltpu.SemaphoreType.DMA((7,)),
            pltpu.SemaphoreType.DMA((5,)),
        ],
        compiler_params=pltpu.CompilerParams(vmem_limit_bytes=56 * 1024 * 1024),
    )(*outs, sol, search, basis)


def solution(mesh):
    torus = Mesh(mesh.devices.reshape(4, 4, 2, 4, 4), (X, Z, C, H, Y))
    maps, image = P(None, ROW, COL), P(ROW, COL)
    return jax.shard_map(
        body,
        mesh=torus,
        in_specs=(maps, maps, maps, image, image, P(), P(), P(), image, image, image),
        out_specs=(maps, maps, maps, image, image),
        check_vma=False,
    )
```

```python
import jax
import jax.numpy as jnp
from jax import lax
from jax.experimental import pallas as pl
from jax.experimental.pallas import tpu as pltpu
from jax.sharding import Mesh
from jax.sharding import PartitionSpec as P

X, Z, C, H, Y = "row_0", "row_1", "row_2", "col_0", "col_1"
ROW = (X, Z, C)
COL = (H, Y)
MESH = pl.DeviceIdType.MESH
f32 = jnp.float32
bf16 = jnp.bfloat16
EPS = 1e-12

K, L, R, W = 8, 512, 64, 128
CL = 5
EXT = CL * W


def ring(a, n):
    return min(a, n - a)


PLANE = [(dx, dy, dc) for dx in range(4) for dy in range(4) for dc in range(2)][1:]
PLANE.sort(key=lambda o: -(ring(o[0], 4) + ring(o[1], 4)))
LINE = sorted(range(1, 16), key=lambda d: -ring(d, 16))


def split(x):
    hi = x.astype(bf16)
    return hi, (x - hi.astype(f32)).astype(bf16)


def dot(a, b, ca, cb):
    return lax.dot_general(a, b, (((ca,), (cb,)), ((), ())), preferred_element_type=f32)


def kernel(
    basis_h, resid_a_h, resid_b_h, scal_h, pa_h, pb_h, mask_h, wcode_h, rcode_h,
    raw_v_h, raw_a_h, raw_b_h, coef_h,
    raw_v, raw_a, raw_b, coef, basis, resid_a, resid_b, scal, pa, pb, mask, wcode, rcode,
    src_r, src_c, ta_hi, ta_lo, tb_hi, tb_lo, to_hi, to_lo, wext_a, wext_b, wext_o,
    even, odd, r1, r2, r3, cp, c1, c2, ext_c, ext_e, ext_o,
    sums_plane, sums_line, send_sem, recv_sem, sum_sem, load_sem, ready,
    square_a, next_square_a, next_a,
):
    x, z, c, h, y = (lax.axis_index(a) for a in (X, Z, C, H, Y))
    started = []

    def core():
        return {C: 1 - c}

    def run(d):
        return {Z: lax.rem(z + d, 4)}

    def across(d):
        return {Z: lax.rem(z + d, 4), X: lax.rem(x + jnp.where(z + d < 4, 3, 1), 4)}

    def along_x(d):
        return {X: lax.rem(x + d, 4)}

    def along_y(d):
        return {Y: lax.rem(y + d, 4)}

    def far(d):
        return {H: lax.rem(h + d, 4)}

    def plane(o):
        return {X: lax.rem(x + o[0], 4), Y: lax.rem(y + o[1], 4), C: lax.rem(c + o[2], 2)}

    def line(d):
        at = 4 * h + z + d
        return {H: lax.rem(at // 4, 4), Z: lax.rem(at, 4)}

    def copy(src, dst, to, again=False):
        i = len(started) - again
        d = pltpu.make_async_remote_copy(
            src_ref=src, dst_ref=dst, send_sem=send_sem.at[i], recv_sem=recv_sem.at[i], device_id=to, device_id_type=MESH
        )
        if not again:
            started.append(d)
        return d

    def share(sums, offsets, to, n):
        rows = sums.at[pl.ds(0, 1)]
        for i, o in enumerate(offsets):
            pltpu.make_async_remote_copy(
                src_ref=rows, dst_ref=sums.at[pl.ds(i + 1, 1)], send_sem=sum_sem.at[n], recv_sem=sum_sem.at[n + 1],
                device_id=to(o), device_id_type=MESH,
            ).start()
        others = sums.at[pl.ds(1, len(offsets))]
        return pltpu.make_async_remote_copy(
            src_ref=others, dst_ref=others, send_sem=sum_sem.at[n], recv_sem=sum_sem.at[n + 1],
            device_id=to(offsets[0]), device_id_type=MESH,
        )

    barrier = pltpu.get_barrier_semaphore()
    peers = [core()] + [run(d) for d in (1, 2, 3)] + [across(d) for d in (1, 2, 3)] + [along_y(d) for d in (1, 2, 3)]
    peers += [along_x(1), along_x(3), far(1), far(3)]
    for to in peers:
        pl.semaphore_signal(barrier, inc=1, device_id=to, device_id_type=MESH)

    pairs = (
        (pa_h, pa), (pb_h, pb), (mask_h, mask), (basis_h, basis), (scal_h, scal), (wcode_h, wcode),
        (rcode_h, rcode), (resid_a_h, resid_a), (resid_b_h, resid_b),
    )
    loads = [pltpu.make_async_copy(a, b, load_sem.at[i]) for i, (a, b) in enumerate(pairs)]
    for s in loads:
        s.start()

    pad = jnp.zeros((1, EXT - L), f32)

    def table(profile, k, rows):
        row = jnp.concatenate([profile[k : k + 1, :], pad], axis=1)
        return split(pltpu.roll(jnp.broadcast_to(row, (rows, EXT)), 0, 1, stride=1, stride_axis=0))

    loads[0].wait()
    for k in range(K):
        ta_hi[k * W : (k + 1) * W, :], ta_lo[k * W : (k + 1) * W, :] = table(pa, k, W)

    loads[2].wait()
    loads[3].wait()
    m = mask[...].astype(f32)
    for k in range(K):
        hi, lo = split(basis[k] * m)
        src_r[0:R, k * W : (k + 1) * W] = hi
        src_r[R : 2 * R, k * W : (k + 1) * W] = lo
        src_c[k * R : (k + 1) * R, 0:W] = hi
        src_c[k * R : (k + 1) * R, W : 2 * W] = lo

    middle = slice(W, EXT - W)
    part = dot(src_r[...], ta_hi[:, middle], 1, 0) + dot(src_r[...], ta_lo[:, middle], 1, 0)
    part = part[:R] + part[R:]
    for level in (1, 2, 3):
        cp[level] = part[:, (level - 1) * W : level * W]
    for level in (0, 4):
        at = slice(level * W, (level + 1) * W)
        part = dot(src_r[...], ta_hi[:, at], 1, 0) + dot(src_r[...], ta_lo[:, at], 1, 0)
        cp[level] = part[:R] + part[R:]
    for s in loads[4:]:
        s.wait()
    alpha = scal[0]
    base = 1.0 / (1.0 + 0.25 * wcode[...].astype(f32))
    weight_a = jnp.where(rcode[...] != 2, base, 0.0)
    weight_b = jnp.where(rcode[...] != 1, base, 0.0)
    loads[1].wait()
    for k in range(K):
        at = slice(k * R, (k + 1) * R)
        hi, lo = table(pb, k, R)
        tb_hi[at, :], tb_lo[at, :] = hi, lo
        for source, dest in ((hi, to_hi), (lo, to_lo)):
            dest[at, :] = jnp.concatenate([source[:, (2 * i + 1) * R : (2 * i + 2) * R] for i in range(4)], axis=1)

    part = dot(tb_hi[...], src_c[...], 0, 0) + dot(tb_lo[...], src_c[...], 0, 0)
    part = part[:, :W] + part[:, W:]
    for level in range(9):
        block = part[level * R : (level + 1) * R]
        if level % 2:
            odd[level // 2] = block
        else:
            even[level // 2] = block
    square_a[...] = weight_a * weight_a

    pl.semaphore_wait(barrier, len(peers))
    s_r1 = copy(odd, r1, core())
    s_r1.start()
    s_c1 = [copy(cp.at[d], c1.at[d], along_y(d)) for d in (2, 1, 3)]
    for s in s_c1:
        s.start()
    s_k1 = copy(square_a, next_square_a, far(3))
    pl.when(h > 0)(s_k1.start)

    s_r1.wait_recv()
    for i in range(4):
        even[1 - c + i] = even[1 - c + i] + r1[i]
    s_r2 = []
    for d in (1, 2, 3):
        inside = z + d < 4
        near = copy(even.at[d], r2.at[d], run(d))
        cross = copy(even.at[d], r2.at[d], across(d), again=True)
        pl.when(inside)(near.start)
        pl.when(jnp.logical_not(inside) & (x < 3))(cross.start)
        s_r2.append((near, (d <= z) | (x > 0), inside | (x < 3)))
    s_r3 = copy(even.at[4], r3, along_x(1))
    pl.when(x < 3)(s_r3.start)

    for s in s_c1:
        s.wait_recv()
    here, there = cp[0], cp[4]
    for d in (1, 2, 3):
        mine = d <= y
        here = here + jnp.where(mine, c1[d], 0.0)
        there = there + jnp.where(mine, 0.0, c1[d])
    beyond = there
    cp[4] = there
    s_c2 = copy(cp.at[4], c2, far(1))
    pl.when(h < 3)(s_c2.start)
    part_a = weight_a * (weight_a * here - alpha * resid_a[...])
    cp[0] = part_a
    s_d1 = copy(cp.at[0], next_a, far(3))
    pl.when(h > 0)(s_d1.start)

    rows_here = even[0]
    for d, (s, comes, _) in enumerate(s_r2, 1):
        pl.when(comes)(s.wait_recv)
        rows_here = rows_here + jnp.where(comes, r2[d], 0.0)
    pl.when(x > 0)(s_r3.wait_recv)
    rows_here = rows_here + jnp.where(x > 0, r3[...], 0.0)
    rb = weight_b * rows_here - alpha * resid_b[...]
    wb = weight_b * rb
    ext_e[0] = wb
    s_a2 = []
    for d in (3, 2, 1):
        inside = z + d >= 4
        near = copy(ext_e.at[0], ext_e.at[4 - d], run(d))
        cross = copy(ext_e.at[0], ext_e.at[4 - d], across(d), again=True)
        pl.when(inside)(near.start)
        pl.when(jnp.logical_not(inside) & (x > 0))(cross.start)
        s_a2.append((near, (z + 4 - d < 4) | (x < 3), inside | (x > 0)))
    s_a1 = copy(ext_e.at[0], ext_e.at[4], along_x(3))
    pl.when(x > 0)(s_a1.start)
    raw_b[...] = rb

    pl.when(h > 0)(s_c2.wait_recv)
    came = jnp.where(h > 0, c2[...], 0.0)
    wa = part_a + square_a[...] * came
    ext_c[0] = wa
    s_d2 = []
    for d in (1, 2, 3):
        to = along_y(d)
        s = copy(ext_c.at[0], ext_c.at[4 - d], to)
        later = copy(ext_c.at[4], ext_c.at[4 - d], to, again=True)
        s_d2.append((s, later, y + d >= 4))
    for s, later, now in s_d2:
        pl.when(now)(s.start)
    ra = weight_a * (here + came) - alpha * resid_a[...]
    raw_a[...] = ra
    pl.when(h < 3)(s_k1.wait_recv)
    pl.when(h < 3)(s_d1.wait_recv)
    ext_c[4] = jnp.where(h < 3, next_a[...] + next_square_a[...] * beyond, 0.0)
    for s, later, now in s_d2:
        pl.when(jnp.logical_not(now))(later.start)
    for d in (1, 2, 3):
        pl.semaphore_signal(ready, inc=1, device_id=run(d), device_id_type=MESH)

    def tile_of(q):
        t = jnp.sum(q.reshape(-1, 8, W), axis=0)
        t = t + pltpu.roll(t, 64, 1)
        return t + pltpu.roll(t, 32, 1)

    rr = tile_of(ra * ra + rb * rb)
    sq = jnp.zeros((R, W), f32)
    for k in range(K):
        sq = sq + basis[k] * basis[k]
    vv = tile_of(sq)

    def put_a(level, block):
        hi, lo = split(block)
        wext_a[0:R, level * W : (level + 1) * W] = hi
        wext_a[R : 2 * R, level * W : (level + 1) * W] = lo

    def put_b(level, block):
        hi, lo = split(block)
        wext_b[level * R : (level + 1) * R, 0:W] = hi
        wext_b[level * R : (level + 1) * R, W : 2 * W] = lo

    put_a(0, wa)
    put_a(4, ext_c[4])
    put_b(0, wb)
    for level in (1, 3, 5, 7, 9):
        wext_b[level * R : (level + 1) * R, :] = jnp.zeros((R, 2 * W), bf16)

    ends = wext_a[:, :W], wext_a[:, EXT - W :]
    tables = ta_hi, ta_lo
    ga = sum(dot(w, t[:, at], 1, 1) for t in tables for w, at in zip(ends, (slice(0, W), slice(EXT - W, EXT))))
    ga = ga[:R] + ga[R:]
    for k in range(K):
        raw_v[k] = ga[:, k * W : (k + 1) * W]
    for level, (s, comes, _) in enumerate(s_a2, 1):
        pl.when(comes)(s.wait_recv)
        ext_e[level] = jnp.where(comes, ext_e[level], 0.0)
    pl.when(x < 3)(s_a1.wait_recv)
    ext_e[4] = jnp.where(x < 3, ext_e[4], 0.0)
    s_a3 = copy(ext_e.at[pl.ds(1 - c, 4)], ext_o, core())
    s_a3.start()
    for d in (1, 2, 3, 4):
        put_b(2 * d, ext_e[d])
    gb = dot(tb_hi[...], wext_b[...], 1, 0) + dot(tb_lo[...], wext_b[...], 1, 0)
    gb = gb[:, :W] + gb[:, W:]
    for k in range(K):
        raw_v[k] = raw_v[k] + gb[k * R : (k + 1) * R]
    for s, _, _ in s_d2:
        s.wait_recv()
    for d in (1, 2, 3):
        put_a(d, ext_c[d])
    ga = dot(wext_a[:, middle], ta_hi[:, middle], 1, 1) + dot(wext_a[:, middle], ta_lo[:, middle], 1, 1)
    ga = ga[:R] + ga[R:]
    for k in range(K):
        raw_v[k] = raw_v[k] + ga[:, k * W : (k + 1) * W]
    s_a3.wait_recv()
    for d in range(4):
        hi, lo = split(ext_o[d])
        wext_o[d * R : (d + 1) * R, 0:W] = hi
        wext_o[d * R : (d + 1) * R, W : 2 * W] = lo
    gb = dot(to_hi[...], wext_o[...], 1, 0) + dot(to_lo[...], wext_o[...], 1, 0)
    gb = gb[:, :W] + gb[:, W:]
    zz = jnp.zeros((R, W), f32)
    zv = jnp.zeros((R, W), f32)
    for k in range(K):
        g = m * (raw_v[k] + gb[k * R : (k + 1) * R])
        raw_v[k] = g
        zz = zz + g * g
        zv = zv + g * basis[k]

    stores = [(raw_v, raw_v_h), (raw_a, raw_a_h), (raw_b, raw_b_h), (coef, coef_h)]
    stores = [pltpu.make_async_copy(a, b, load_sem.at[i]) for i, (a, b) in enumerate(stores)]

    quarter = lax.broadcasted_iota(jnp.int32, (8, W), 1) // (W // 4)
    both = jnp.where(quarter == 0, rr, vv)
    tile = jnp.where(quarter == 2, tile_of(zz), jnp.where(quarter == 3, tile_of(zv), both))
    sums_plane[0:1, :] = jnp.sum(tile, axis=0, keepdims=True)
    group_plane = share(sums_plane, PLANE, plane, 0)
    for s in stores[:3]:
        s.start()
    sent = {id(s_c2): h < 3, id(s_r3): x < 3, id(s_d1): h > 0, id(s_a1): x > 0, id(s_k1): h > 0}
    sent.update((id(s), goes) for s, _, goes in s_r2 + s_a2)
    for s in started:
        pl.when(sent.get(id(s), True))(s.wait_send)
    group_plane.wait_recv()
    sums_line[0:1, :] = jnp.sum(sums_plane[...], axis=0, keepdims=True)
    pl.semaphore_wait(ready, 3)
    group_line = share(sums_line, LINE, line, 2)
    group_plane.wait_send()
    for s in stores[:3]:
        s.wait()
    group_line.wait_recv()
    row = jnp.sum(sums_line[...], axis=0, keepdims=True)
    mine = quarter == lax.broadcasted_iota(jnp.int32, (8, W), 0)
    sums = jnp.sum(jnp.where(mine, row, 0.0), axis=1, keepdims=True)
    phibar, rhobar = scal[1], scal[2]
    beta_square = sums[0:1] + EPS
    inv_beta = lax.rsqrt(beta_square)
    inv_rho_square = 1.0 / (rhobar * rhobar + beta_square)
    beta = beta_square * inv_beta
    alpha_square = sums[2:3] * (inv_beta * inv_beta) - 2.0 * sums[3:4] + beta_square * sums[1:2] + EPS
    inv_alpha = lax.rsqrt(alpha_square)
    alpha_next = alpha_square * inv_alpha
    step = rhobar * phibar * inv_rho_square
    values = (inv_beta, inv_beta * inv_alpha, beta * inv_alpha, step, beta * alpha_next * inv_rho_square)
    for i, value in enumerate(values):
        coef[i : i + 1, :] = jnp.broadcast_to(value, (1, W))
    coef[5:8, :] = jnp.zeros((3, W), f32)
    stores[3].start()
    group_line.wait_send()
    stores[3].wait()


N_COPIES = 19


def finish(
    grad_h, raw_a_h, raw_b_h, coef_h, sol_h, search_h, basis_h,
    sol_o, search_o, basis_o, resid_a_o, resid_b_o,
    grad, raw_a, raw_b, coef, sol, search, basis, load_sem, store_sem,
):
    pairs = (
        (coef_h, coef), (search_h, search), (sol_h, sol), (grad_h, grad), (basis_h, basis), (raw_a_h, raw_a), (raw_b_h, raw_b),
    )
    loads = [pltpu.make_async_copy(a, b, load_sem.at[i]) for i, (a, b) in enumerate(pairs)]
    for s in loads:
        s.start()
    pairs = ((sol, sol_o), (grad, basis_o), (search, search_o), (raw_a, resid_a_o), (raw_b, resid_b_o))
    stores = [pltpu.make_async_copy(a, b, store_sem.at[i]) for i, (a, b) in enumerate(pairs)]
    for s in loads[:3]:
        s.wait()
    inv_beta, scale, shift = coef[0:1, :], coef[1:2, :], coef[2:3, :]
    step, turn = coef[3:4, :], coef[4:5, :]
    sol[...] = sol[...] + step * search[...]
    stores[0].start()
    for s in loads[3:5]:
        s.wait()
    v = grad[...] * scale - shift * basis[...]
    grad[...] = v
    stores[1].start()
    search[...] = v - turn * search[...]
    stores[2].start()
    for s in loads[5:]:
        s.wait()
    raw_a[...] = raw_a[...] * inv_beta
    stores[3].start()
    raw_b[...] = raw_b[...] * inv_beta
    stores[4].start()
    for s in stores:
        s.wait()


def body(sol, search, basis, resid_a, resid_b, scal, pa, pb, mask, wcode, rcode):
    hbm = pl.BlockSpec(memory_space=pltpu.HBM)
    image = jax.ShapeDtypeStruct((R, W), f32)
    maps = jax.ShapeDtypeStruct((K, R, W), f32)
    words = pltpu.VMEM((R, W), jnp.int32)
    outs = pl.pallas_call(
        kernel,
        out_shape=(maps, image, image, jax.ShapeDtypeStruct((8, W), f32)),
        in_specs=[hbm] * 9,
        out_specs=(hbm,) * 4,
        scratch_shapes=[
            pltpu.VMEM((K, R, W), f32),
            pltpu.VMEM((R, W), f32),
            pltpu.VMEM((R, W), f32),
            pltpu.VMEM((8, W), f32),
            pltpu.VMEM((K, R, W), f32),
            pltpu.VMEM((R, W), f32),
            pltpu.VMEM((R, W), f32),
            pltpu.SMEM((3,), f32),
            pltpu.VMEM((K, L), f32),
            pltpu.VMEM((K, L), f32),
            words,
            words,
            words,
            pltpu.VMEM((2 * R, K * W), bf16),
            pltpu.VMEM((K * R, 2 * W), bf16),
            pltpu.VMEM((K * W, EXT), bf16),
            pltpu.VMEM((K * W, EXT), bf16),
            pltpu.VMEM((K * R, EXT), bf16),
            pltpu.VMEM((K * R, EXT), bf16),
            pltpu.VMEM((K * R, 4 * R), bf16),
            pltpu.VMEM((K * R, 4 * R), bf16),
            pltpu.VMEM((2 * R, EXT), bf16),
            pltpu.VMEM((EXT, 2 * W), bf16),
            pltpu.VMEM((4 * R, 2 * W), bf16),
            pltpu.VMEM((5, R, W), f32),
            pltpu.VMEM((4, R, W), f32),
            pltpu.VMEM((4, R, W), f32),
            pltpu.VMEM((4, R, W), f32),
            pltpu.VMEM((R, W), f32),
            pltpu.VMEM((5, R, W), f32),
            pltpu.VMEM((4, R, W), f32),
            pltpu.VMEM((R, W), f32),
            pltpu.VMEM((5, R, W), f32),
            pltpu.VMEM((5, R, W), f32),
            pltpu.VMEM((4, R, W), f32),
            pltpu.VMEM((1 + len(PLANE), W), f32),
            pltpu.VMEM((1 + len(LINE), W), f32),
            pltpu.SemaphoreType.DMA((N_COPIES,)),
            pltpu.SemaphoreType.DMA((N_COPIES,)),
            pltpu.SemaphoreType.DMA((4,)),
            pltpu.SemaphoreType.DMA((9,)),
            pltpu.SemaphoreType.REGULAR,
            *[pltpu.VMEM((R, W), f32)] * 3,
        ],
        compiler_params=pltpu.CompilerParams(
            collective_id=0, has_side_effects=True, vmem_limit_bytes=56 * 1024 * 1024
        ),
    )(basis, resid_a, resid_b, scal, pa, pb, mask, wcode, rcode)
    return pl.pallas_call(
        finish,
        out_shape=(maps, maps, maps, image, image),
        in_specs=[hbm] * 7,
        out_specs=(hbm,) * 5,
        scratch_shapes=[
            pltpu.VMEM((K, R, W), f32),
            pltpu.VMEM((R, W), f32),
            pltpu.VMEM((R, W), f32),
            pltpu.VMEM((8, W), f32),
            pltpu.VMEM((K, R, W), f32),
            pltpu.VMEM((K, R, W), f32),
            pltpu.VMEM((K, R, W), f32),
            pltpu.SemaphoreType.DMA((7,)),
            pltpu.SemaphoreType.DMA((5,)),
        ],
        compiler_params=pltpu.CompilerParams(vmem_limit_bytes=56 * 1024 * 1024),
    )(*outs, sol, search, basis)


def solution(mesh):
    torus = Mesh(mesh.devices.reshape(4, 4, 2, 4, 4), (X, Z, C, H, Y))
    maps, image = P(None, ROW, COL), P(ROW, COL)
    return jax.shard_map(
        body,
        mesh=torus,
        in_specs=(maps, maps, maps, image, image, P(), P(), P(), image, image, image),
        out_specs=(maps, maps, maps, image, image),
        check_vma=False,
    )
```

```python
import jax
import jax.numpy as jnp
from jax import lax
from jax.experimental import pallas as pl
from jax.experimental.pallas import tpu as pltpu
from jax.sharding import Mesh
from jax.sharding import PartitionSpec as P

X, Z, C, H, Y = "row_0", "row_1", "row_2", "col_0", "col_1"
ROW = (X, Z, C)
COL = (H, Y)
MESH = pl.DeviceIdType.MESH
f32 = jnp.float32
bf16 = jnp.bfloat16
EPS = 1e-12

K, L, R, W = 8, 512, 64, 128
CL = 5
EXT = CL * W


def ring(a, n):
    return min(a, n - a)


PLANE = [(dx, dy, dc) for dx in range(4) for dy in range(4) for dc in range(2)][1:]
PLANE.sort(key=lambda o: -(ring(o[0], 4) + ring(o[1], 4)))
LINE = sorted(range(1, 16), key=lambda d: -ring(d, 16))


def split(x):
    hi = x.astype(bf16)
    return hi, (x - hi.astype(f32)).astype(bf16)


def dot(a, b, ca, cb):
    return lax.dot_general(a, b, (((ca,), (cb,)), ((), ())), preferred_element_type=f32)


def kernel(
    basis_h, resid_a_h, resid_b_h, scal_h, pa_h, pb_h, mask_h, wcode_h, rcode_h,
    raw_v_h, raw_a_h, raw_b_h, coef_h,
    raw_v, raw_a, raw_b, coef, basis, resid_a, resid_b, scal, pa, pb, mask, wcode, rcode,
    src_r, src_c, ta_hi, ta_lo, tb_hi, tb_lo, to_hi, to_lo, wext_a, wext_b, wext_o,
    even, odd, r1, r2, r3, cp, c1, c2, ext_c, ext_e, ext_o,
    sums_plane, sums_line, send_sem, recv_sem, sum_sem, load_sem, ready,
    square_a, next_square_a, next_a,
):
    x, z, c, h, y = (lax.axis_index(a) for a in (X, Z, C, H, Y))
    started = []

    def core():
        return {C: 1 - c}

    def run(d):
        return {Z: lax.rem(z + d, 4)}

    def across(d):
        return {Z: lax.rem(z + d, 4), X: lax.rem(x + jnp.where(z + d < 4, 3, 1), 4)}

    def along_x(d):
        return {X: lax.rem(x + d, 4)}

    def along_y(d):
        return {Y: lax.rem(y + d, 4)}

    def far(d):
        return {H: lax.rem(h + d, 4)}

    def plane(o):
        return {X: lax.rem(x + o[0], 4), Y: lax.rem(y + o[1], 4), C: lax.rem(c + o[2], 2)}

    def line(d):
        at = 4 * h + z + d
        return {H: lax.rem(at // 4, 4), Z: lax.rem(at, 4)}

    def copy(src, dst, to, again=False):
        i = len(started) - again
        d = pltpu.make_async_remote_copy(
            src_ref=src, dst_ref=dst, send_sem=send_sem.at[i], recv_sem=recv_sem.at[i], device_id=to, device_id_type=MESH
        )
        if not again:
            started.append(d)
        return d

    def share(sums, offsets, to, n):
        rows = sums.at[pl.ds(0, 1)]
        for i, o in enumerate(offsets):
            pltpu.make_async_remote_copy(
                src_ref=rows, dst_ref=sums.at[pl.ds(i + 1, 1)], send_sem=sum_sem.at[n], recv_sem=sum_sem.at[n + 1],
                device_id=to(o), device_id_type=MESH,
            ).start()
        others = sums.at[pl.ds(1, len(offsets))]
        return pltpu.make_async_remote_copy(
            src_ref=others, dst_ref=others, send_sem=sum_sem.at[n], recv_sem=sum_sem.at[n + 1],
            device_id=to(offsets[0]), device_id_type=MESH,
        )

    barrier = pltpu.get_barrier_semaphore()
    peers = [core()] + [run(d) for d in (1, 2, 3)] + [across(d) for d in (1, 2, 3)] + [along_y(d) for d in (1, 2, 3)]
    peers += [along_x(1), along_x(3), far(1), far(3)]
    for to in peers:
        pl.semaphore_signal(barrier, inc=1, device_id=to, device_id_type=MESH)

    pairs = (
        (pa_h, pa), (pb_h, pb), (mask_h, mask), (basis_h, basis), (scal_h, scal), (wcode_h, wcode),
        (rcode_h, rcode), (resid_a_h, resid_a), (resid_b_h, resid_b),
    )
    loads = [pltpu.make_async_copy(a, b, load_sem.at[i]) for i, (a, b) in enumerate(pairs)]
    for s in loads:
        s.start()

    pad = jnp.zeros((1, EXT - L), f32)

    def table(profile, k, rows):
        row = jnp.concatenate([profile[k : k + 1, :], pad], axis=1)
        return split(pltpu.roll(jnp.broadcast_to(row, (rows, EXT)), 0, 1, stride=1, stride_axis=0))

    loads[0].wait()
    for k in range(K):
        ta_hi[k * W : (k + 1) * W, :], ta_lo[k * W : (k + 1) * W, :] = table(pa, k, W)

    loads[2].wait()
    loads[3].wait()
    m = mask[...].astype(f32)
    for k in range(K):
        hi, lo = split(basis[k] * m)
        src_r[0:R, k * W : (k + 1) * W] = hi
        src_r[R : 2 * R, k * W : (k + 1) * W] = lo
        src_c[k * R : (k + 1) * R, 0:W] = hi
        src_c[k * R : (k + 1) * R, W : 2 * W] = lo

    middle = slice(W, EXT - W)
    part = dot(src_r[...], ta_hi[:, middle], 1, 0) + dot(src_r[...], ta_lo[:, middle], 1, 0)
    part = part[:R] + part[R:]
    for level in (1, 2, 3):
        cp[level] = part[:, (level - 1) * W : level * W]
    for level in (0, 4):
        at = slice(level * W, (level + 1) * W)
        part = dot(src_r[...], ta_hi[:, at], 1, 0) + dot(src_r[...], ta_lo[:, at], 1, 0)
        cp[level] = part[:R] + part[R:]
    for s in loads[4:]:
        s.wait()
    alpha = scal[0]
    base = 1.0 / (1.0 + 0.25 * wcode[...].astype(f32))
    weight_a = jnp.where(rcode[...] != 2, base, 0.0)
    weight_b = jnp.where(rcode[...] != 1, base, 0.0)
    loads[1].wait()
    for k in range(K):
        at = slice(k * R, (k + 1) * R)
        hi, lo = table(pb, k, R)
        tb_hi[at, :], tb_lo[at, :] = hi, lo
        for source, dest in ((hi, to_hi), (lo, to_lo)):
            dest[at, :] = jnp.concatenate([source[:, (2 * i + 1) * R : (2 * i + 2) * R] for i in range(4)], axis=1)

    part = dot(tb_hi[...], src_c[...], 0, 0) + dot(tb_lo[...], src_c[...], 0, 0)
    part = part[:, :W] + part[:, W:]
    for level in range(9):
        block = part[level * R : (level + 1) * R]
        if level % 2:
            odd[level // 2] = block
        else:
            even[level // 2] = block
    square_a[...] = weight_a * weight_a

    pl.semaphore_wait(barrier, len(peers))
    s_r1 = copy(odd, r1, core())
    s_r1.start()
    s_c1 = [copy(cp.at[d], c1.at[d], along_y(d)) for d in (2, 1, 3)]
    for s in s_c1:
        s.start()
    s_k1 = copy(square_a, next_square_a, far(3))
    pl.when(h > 0)(s_k1.start)

    s_r1.wait_recv()
    for i in range(4):
        even[1 - c + i] = even[1 - c + i] + r1[i]
    s_r2 = []
    for d in (1, 2, 3):
        inside = z + d < 4
        near = copy(even.at[d], r2.at[d], run(d))
        cross = copy(even.at[d], r2.at[d], across(d), again=True)
        pl.when(inside)(near.start)
        pl.when(jnp.logical_not(inside) & (x < 3))(cross.start)
        s_r2.append((near, (d <= z) | (x > 0), inside | (x < 3)))
    s_r3 = copy(even.at[4], r3, along_x(1))
    pl.when(x < 3)(s_r3.start)

    for s in s_c1:
        s.wait_recv()
    here, there = cp[0], cp[4]
    for d in (1, 2, 3):
        mine = d <= y
        here = here + jnp.where(mine, c1[d], 0.0)
        there = there + jnp.where(mine, 0.0, c1[d])
    beyond = there
    cp[4] = there
    s_c2 = copy(cp.at[4], c2, far(1))
    pl.when(h < 3)(s_c2.start)
    part_a = weight_a * (weight_a * here - alpha * resid_a[...])
    cp[0] = part_a
    s_d1 = copy(cp.at[0], next_a, far(3))
    pl.when(h > 0)(s_d1.start)

    rows_here = even[0]
    for d, (s, comes, _) in enumerate(s_r2, 1):
        pl.when(comes)(s.wait_recv)
        rows_here = rows_here + jnp.where(comes, r2[d], 0.0)
    pl.when(x > 0)(s_r3.wait_recv)
    rows_here = rows_here + jnp.where(x > 0, r3[...], 0.0)
    rb = weight_b * rows_here - alpha * resid_b[...]
    wb = weight_b * rb
    ext_e[0] = wb
    s_a2 = []
    for d in (3, 2, 1):
        inside = z + d >= 4
        near = copy(ext_e.at[0], ext_e.at[4 - d], run(d))
        cross = copy(ext_e.at[0], ext_e.at[4 - d], across(d), again=True)
        pl.when(inside)(near.start)
        pl.when(jnp.logical_not(inside) & (x > 0))(cross.start)
        s_a2.append((near, (z + 4 - d < 4) | (x < 3), inside | (x > 0)))
    s_a1 = copy(ext_e.at[0], ext_e.at[4], along_x(3))
    pl.when(x > 0)(s_a1.start)
    raw_b[...] = rb

    pl.when(h > 0)(s_c2.wait_recv)
    came = jnp.where(h > 0, c2[...], 0.0)
    wa = part_a + square_a[...] * came
    ext_c[0] = wa
    s_d2 = []
    for d in (1, 2, 3):
        to = along_y(d)
        s = copy(ext_c.at[0], ext_c.at[4 - d], to)
        later = copy(ext_c.at[4], ext_c.at[4 - d], to, again=True)
        s_d2.append((s, later, y + d >= 4))
    for s, later, now in s_d2:
        pl.when(now)(s.start)
    ra = weight_a * (here + came) - alpha * resid_a[...]
    raw_a[...] = ra
    pl.when(h < 3)(s_k1.wait_recv)
    pl.when(h < 3)(s_d1.wait_recv)
    ext_c[4] = jnp.where(h < 3, next_a[...] + next_square_a[...] * beyond, 0.0)
    for s, later, now in s_d2:
        pl.when(jnp.logical_not(now))(later.start)
    for d in (1, 2, 3):
        pl.semaphore_signal(ready, inc=1, device_id=run(d), device_id_type=MESH)

    def tile_of(q):
        t = jnp.sum(q.reshape(-1, 8, W), axis=0)
        t = t + pltpu.roll(t, 64, 1)
        return t + pltpu.roll(t, 32, 1)

    rr = tile_of(ra * ra + rb * rb)
    sq = jnp.zeros((R, W), f32)
    for k in range(K):
        sq = sq + basis[k] * basis[k]
    vv = tile_of(sq)

    def put_a(level, block):
        hi, lo = split(block)
        wext_a[0:R, level * W : (level + 1) * W] = hi
        wext_a[R : 2 * R, level * W : (level + 1) * W] = lo

    def put_b(level, block):
        hi, lo = split(block)
        wext_b[level * R : (level + 1) * R, 0:W] = hi
        wext_b[level * R : (level + 1) * R, W : 2 * W] = lo

    put_a(0, wa)
    put_a(4, ext_c[4])
    put_b(0, wb)
    for level in (1, 3, 5, 7, 9):
        wext_b[level * R : (level + 1) * R, :] = jnp.zeros((R, 2 * W), bf16)

    ends = wext_a[:, :W], wext_a[:, EXT - W :]
    tables = ta_hi, ta_lo
    ga = sum(dot(w, t[:, at], 1, 1) for t in tables for w, at in zip(ends, (slice(0, W), slice(EXT - W, EXT))))
    ga = ga[:R] + ga[R:]
    for k in range(K):
        raw_v[k] = ga[:, k * W : (k + 1) * W]
    for level, (s, comes, _) in enumerate(s_a2, 1):
        pl.when(comes)(s.wait_recv)
        ext_e[level] = jnp.where(comes, ext_e[level], 0.0)
    pl.when(x < 3)(s_a1.wait_recv)
    ext_e[4] = jnp.where(x < 3, ext_e[4], 0.0)
    s_a3 = copy(ext_e.at[pl.ds(1 - c, 4)], ext_o, core())
    s_a3.start()
    for d in (1, 2, 3, 4):
        put_b(2 * d, ext_e[d])
    gb = dot(tb_hi[...], wext_b[...], 1, 0) + dot(tb_lo[...], wext_b[...], 1, 0)
    gb = gb[:, :W] + gb[:, W:]
    for k in range(K):
        raw_v[k] = raw_v[k] + gb[k * R : (k + 1) * R]
    s_a3.wait_recv()
    for d in range(4):
        hi, lo = split(ext_o[d])
        wext_o[d * R : (d + 1) * R, 0:W] = hi
        wext_o[d * R : (d + 1) * R, W : 2 * W] = lo
    gb = dot(to_hi[...], wext_o[...], 1, 0) + dot(to_lo[...], wext_o[...], 1, 0)
    gb = gb[:, :W] + gb[:, W:]
    for k in range(K):
        raw_v[k] = raw_v[k] + gb[k * R : (k + 1) * R]
    for s, _, _ in s_d2:
        s.wait_recv()
    for d in (1, 2, 3):
        put_a(d, ext_c[d])
    ga = dot(wext_a[:, middle], ta_hi[:, middle], 1, 1) + dot(wext_a[:, middle], ta_lo[:, middle], 1, 1)
    ga = ga[:R] + ga[R:]
    zz = jnp.zeros((R, W), f32)
    zv = jnp.zeros((R, W), f32)
    for k in range(K):
        g = m * (raw_v[k] + ga[:, k * W : (k + 1) * W])
        raw_v[k] = g
        zz = zz + g * g
        zv = zv + g * basis[k]

    stores = [(raw_v, raw_v_h), (raw_a, raw_a_h), (raw_b, raw_b_h), (coef, coef_h)]
    stores = [pltpu.make_async_copy(a, b, load_sem.at[i]) for i, (a, b) in enumerate(stores)]

    quarter = lax.broadcasted_iota(jnp.int32, (8, W), 1) // (W // 4)
    both = jnp.where(quarter == 0, rr, vv)
    tile = jnp.where(quarter == 2, tile_of(zz), jnp.where(quarter == 3, tile_of(zv), both))
    sums_plane[0:1, :] = jnp.sum(tile, axis=0, keepdims=True)
    group_plane = share(sums_plane, PLANE, plane, 0)
    for s in stores[:3]:
        s.start()
    sent = {id(s_c2): h < 3, id(s_r3): x < 3, id(s_d1): h > 0, id(s_a1): x > 0, id(s_k1): h > 0}
    sent.update((id(s), goes) for s, _, goes in s_r2 + s_a2)
    for s in started:
        pl.when(sent.get(id(s), True))(s.wait_send)
    group_plane.wait_recv()
    sums_line[0:1, :] = jnp.sum(sums_plane[...], axis=0, keepdims=True)
    pl.semaphore_wait(ready, 3)
    group_line = share(sums_line, LINE, line, 2)
    group_plane.wait_send()
    for s in stores[:3]:
        s.wait()
    group_line.wait_recv()
    row = jnp.sum(sums_line[...], axis=0, keepdims=True)
    mine = quarter == lax.broadcasted_iota(jnp.int32, (8, W), 0)
    sums = jnp.sum(jnp.where(mine, row, 0.0), axis=1, keepdims=True)
    phibar, rhobar = scal[1], scal[2]
    beta_square = sums[0:1] + EPS
    inv_beta = lax.rsqrt(beta_square)
    inv_rho_square = 1.0 / (rhobar * rhobar + beta_square)
    beta = beta_square * inv_beta
    alpha_square = sums[2:3] * (inv_beta * inv_beta) - 2.0 * sums[3:4] + beta_square * sums[1:2] + EPS
    inv_alpha = lax.rsqrt(alpha_square)
    alpha_next = alpha_square * inv_alpha
    step = rhobar * phibar * inv_rho_square
    values = (inv_beta, inv_beta * inv_alpha, beta * inv_alpha, step, beta * alpha_next * inv_rho_square)
    for i, value in enumerate(values):
        coef[i : i + 1, :] = jnp.broadcast_to(value, (1, W))
    coef[5:8, :] = jnp.zeros((3, W), f32)
    stores[3].start()
    group_line.wait_send()
    stores[3].wait()


N_COPIES = 19


def finish(
    grad_h, raw_a_h, raw_b_h, coef_h, sol_h, search_h, basis_h,
    sol_o, search_o, basis_o, resid_a_o, resid_b_o,
    grad, raw_a, raw_b, coef, sol, search, basis, load_sem, store_sem,
):
    pairs = (
        (coef_h, coef), (search_h, search), (sol_h, sol), (grad_h, grad), (basis_h, basis), (raw_a_h, raw_a), (raw_b_h, raw_b),
    )
    loads = [pltpu.make_async_copy(a, b, load_sem.at[i]) for i, (a, b) in enumerate(pairs)]
    for s in loads:
        s.start()
    pairs = ((sol, sol_o), (grad, basis_o), (search, search_o), (raw_a, resid_a_o), (raw_b, resid_b_o))
    stores = [pltpu.make_async_copy(a, b, store_sem.at[i]) for i, (a, b) in enumerate(pairs)]
    for s in loads[:3]:
        s.wait()
    inv_beta, scale, shift = coef[0:1, :], coef[1:2, :], coef[2:3, :]
    step, turn = coef[3:4, :], coef[4:5, :]
    sol[...] = sol[...] + step * search[...]
    stores[0].start()
    for s in loads[3:5]:
        s.wait()
    v = grad[...] * scale - shift * basis[...]
    grad[...] = v
    stores[1].start()
    search[...] = v - turn * search[...]
    stores[2].start()
    for s in loads[5:]:
        s.wait()
    raw_a[...] = raw_a[...] * inv_beta
    stores[3].start()
    raw_b[...] = raw_b[...] * inv_beta
    stores[4].start()
    for s in stores:
        s.wait()


def body(sol, search, basis, resid_a, resid_b, scal, pa, pb, mask, wcode, rcode):
    hbm = pl.BlockSpec(memory_space=pltpu.HBM)
    image = jax.ShapeDtypeStruct((R, W), f32)
    maps = jax.ShapeDtypeStruct((K, R, W), f32)
    words = pltpu.VMEM((R, W), jnp.int32)
    outs = pl.pallas_call(
        kernel,
        out_shape=(maps, image, image, jax.ShapeDtypeStruct((8, W), f32)),
        in_specs=[hbm] * 9,
        out_specs=(hbm,) * 4,
        scratch_shapes=[
            pltpu.VMEM((K, R, W), f32),
            pltpu.VMEM((R, W), f32),
            pltpu.VMEM((R, W), f32),
            pltpu.VMEM((8, W), f32),
            pltpu.VMEM((K, R, W), f32),
            pltpu.VMEM((R, W), f32),
            pltpu.VMEM((R, W), f32),
            pltpu.SMEM((3,), f32),
            pltpu.VMEM((K, L), f32),
            pltpu.VMEM((K, L), f32),
            words,
            words,
            words,
            pltpu.VMEM((2 * R, K * W), bf16),
            pltpu.VMEM((K * R, 2 * W), bf16),
            pltpu.VMEM((K * W, EXT), bf16),
            pltpu.VMEM((K * W, EXT), bf16),
            pltpu.VMEM((K * R, EXT), bf16),
            pltpu.VMEM((K * R, EXT), bf16),
            pltpu.VMEM((K * R, 4 * R), bf16),
            pltpu.VMEM((K * R, 4 * R), bf16),
            pltpu.VMEM((2 * R, EXT), bf16),
            pltpu.VMEM((EXT, 2 * W), bf16),
            pltpu.VMEM((4 * R, 2 * W), bf16),
            pltpu.VMEM((5, R, W), f32),
            pltpu.VMEM((4, R, W), f32),
            pltpu.VMEM((4, R, W), f32),
            pltpu.VMEM((4, R, W), f32),
            pltpu.VMEM((R, W), f32),
            pltpu.VMEM((5, R, W), f32),
            pltpu.VMEM((4, R, W), f32),
            pltpu.VMEM((R, W), f32),
            pltpu.VMEM((5, R, W), f32),
            pltpu.VMEM((5, R, W), f32),
            pltpu.VMEM((4, R, W), f32),
            pltpu.VMEM((1 + len(PLANE), W), f32),
            pltpu.VMEM((1 + len(LINE), W), f32),
            pltpu.SemaphoreType.DMA((N_COPIES,)),
            pltpu.SemaphoreType.DMA((N_COPIES,)),
            pltpu.SemaphoreType.DMA((4,)),
            pltpu.SemaphoreType.DMA((9,)),
            pltpu.SemaphoreType.REGULAR,
            *[pltpu.VMEM((R, W), f32)] * 3,
        ],
        compiler_params=pltpu.CompilerParams(
            collective_id=0, has_side_effects=True, vmem_limit_bytes=56 * 1024 * 1024
        ),
    )(basis, resid_a, resid_b, scal, pa, pb, mask, wcode, rcode)
    return pl.pallas_call(
        finish,
        out_shape=(maps, maps, maps, image, image),
        in_specs=[hbm] * 7,
        out_specs=(hbm,) * 5,
        scratch_shapes=[
            pltpu.VMEM((K, R, W), f32),
            pltpu.VMEM((R, W), f32),
            pltpu.VMEM((R, W), f32),
            pltpu.VMEM((8, W), f32),
            pltpu.VMEM((K, R, W), f32),
            pltpu.VMEM((K, R, W), f32),
            pltpu.VMEM((K, R, W), f32),
            pltpu.SemaphoreType.DMA((7,)),
            pltpu.SemaphoreType.DMA((5,)),
        ],
        compiler_params=pltpu.CompilerParams(vmem_limit_bytes=56 * 1024 * 1024),
    )(*outs, sol, search, basis)


def solution(mesh):
    torus = Mesh(mesh.devices.reshape(4, 4, 2, 4, 4), (X, Z, C, H, Y))
    maps, image = P(None, ROW, COL), P(ROW, COL)
    return jax.shard_map(
        body,
        mesh=torus,
        in_specs=(maps, maps, maps, image, image, P(), P(), P(), image, image, image),
        out_specs=(maps, maps, maps, image, image),
        check_vma=False,
    )
```

```python
import jax
import jax.numpy as jnp
from jax import lax
from jax.experimental import pallas as pl
from jax.experimental.pallas import tpu as pltpu
from jax.sharding import Mesh
from jax.sharding import PartitionSpec as P

X, Z, C, H, Y = "row_0", "row_1", "row_2", "col_0", "col_1"
ROW = (X, Z, C)
COL = (H, Y)
MESH = pl.DeviceIdType.MESH
f32 = jnp.float32
bf16 = jnp.bfloat16
EPS = 1e-12

K, L, R, W = 8, 512, 64, 128
CL = 5
EXT = CL * W


def ring(a, n):
    return min(a, n - a)


PLANE = [(dx, dy, dc) for dx in range(4) for dy in range(4) for dc in range(2)][1:]
PLANE.sort(key=lambda o: -(ring(o[0], 4) + ring(o[1], 4)))
LINE = sorted(range(1, 16), key=lambda d: -ring(d, 16))


def split(x):
    hi = x.astype(bf16)
    return hi, (x - hi.astype(f32)).astype(bf16)


def dot(a, b, ca, cb):
    return lax.dot_general(a, b, (((ca,), (cb,)), ((), ())), preferred_element_type=f32)


def kernel(
    basis_h, resid_a_h, resid_b_h, scal_h, pa_h, pb_h, mask_h, wcode_h, rcode_h,
    raw_v_h, raw_a_h, raw_b_h, coef_h,
    raw_v, raw_a, raw_b, coef, basis, resid_a, resid_b, scal, pa, pb, mask, wcode, rcode,
    src_r, src_c, ta_hi, ta_lo, tb_hi, tb_lo, to_hi, to_lo, wext_a, wext_b, wext_o,
    even, odd, r1, r2, r3, cp, c1, c2, ext_c, ext_e, ext_o,
    sums_plane, sums_line, send_sem, recv_sem, sum_sem, load_sem, ready,
    square_a, next_square_a, next_a,
):
    x, z, c, h, y = (lax.axis_index(a) for a in (X, Z, C, H, Y))
    started = []

    def core():
        return {C: 1 - c}

    def run(d):
        return {Z: lax.rem(z + d, 4)}

    def across(d):
        return {Z: lax.rem(z + d, 4), X: lax.rem(x + jnp.where(z + d < 4, 3, 1), 4)}

    def along_x(d):
        return {X: lax.rem(x + d, 4)}

    def along_y(d):
        return {Y: lax.rem(y + d, 4)}

    def far(d):
        return {H: lax.rem(h + d, 4)}

    def plane(o):
        return {X: lax.rem(x + o[0], 4), Y: lax.rem(y + o[1], 4), C: lax.rem(c + o[2], 2)}

    def line(d):
        at = 4 * h + z + d
        return {H: lax.rem(at // 4, 4), Z: lax.rem(at, 4)}

    def copy(src, dst, to, again=False):
        i = len(started) - again
        d = pltpu.make_async_remote_copy(
            src_ref=src, dst_ref=dst, send_sem=send_sem.at[i], recv_sem=recv_sem.at[i], device_id=to, device_id_type=MESH
        )
        if not again:
            started.append(d)
        return d

    def share(sums, offsets, to, n):
        rows = sums.at[pl.ds(0, 1)]
        for i, o in enumerate(offsets):
            pltpu.make_async_remote_copy(
                src_ref=rows, dst_ref=sums.at[pl.ds(i + 1, 1)], send_sem=sum_sem.at[n], recv_sem=sum_sem.at[n + 1],
                device_id=to(o), device_id_type=MESH,
            ).start()
        others = sums.at[pl.ds(1, len(offsets))]
        return pltpu.make_async_remote_copy(
            src_ref=others, dst_ref=others, send_sem=sum_sem.at[n], recv_sem=sum_sem.at[n + 1],
            device_id=to(offsets[0]), device_id_type=MESH,
        )

    barrier = pltpu.get_barrier_semaphore()
    peers = [core()] + [run(d) for d in (1, 2, 3)] + [across(d) for d in (1, 2, 3)] + [along_y(d) for d in (1, 2, 3)]
    peers += [along_x(1), along_x(3), far(1), far(3)]
    for to in peers:
        pl.semaphore_signal(barrier, inc=1, device_id=to, device_id_type=MESH)

    pairs = (
        (pa_h, pa), (pb_h, pb), (mask_h, mask), (basis_h, basis), (scal_h, scal), (wcode_h, wcode),
        (rcode_h, rcode), (resid_a_h, resid_a), (resid_b_h, resid_b),
    )
    loads = [pltpu.make_async_copy(a, b, load_sem.at[i]) for i, (a, b) in enumerate(pairs)]
    for s in loads:
        s.start()

    pad = jnp.zeros((1, EXT - L), f32)

    def table(profile, k, rows):
        row = jnp.concatenate([profile[k : k + 1, :], pad], axis=1)
        return split(pltpu.roll(jnp.broadcast_to(row, (rows, EXT)), 0, 1, stride=1, stride_axis=0))

    loads[0].wait()
    for k in range(K):
        ta_hi[k * W : (k + 1) * W, :], ta_lo[k * W : (k + 1) * W, :] = table(pa, k, W)

    loads[2].wait()
    loads[3].wait()
    m = mask[...].astype(f32)
    for k in range(K):
        hi, lo = split(basis[k] * m)
        src_r[0:R, k * W : (k + 1) * W] = hi
        src_r[R : 2 * R, k * W : (k + 1) * W] = lo
        src_c[k * R : (k + 1) * R, 0:W] = hi
        src_c[k * R : (k + 1) * R, W : 2 * W] = lo

    middle = slice(W, EXT - W)
    part = dot(src_r[...], ta_hi[:, middle], 1, 0) + dot(src_r[...], ta_lo[:, middle], 1, 0)
    part = part[:R] + part[R:]
    for level in (1, 2, 3):
        cp[level] = part[:, (level - 1) * W : level * W]
    for level in (0, 4):
        at = slice(level * W, (level + 1) * W)
        part = dot(src_r[...], ta_hi[:, at], 1, 0) + dot(src_r[...], ta_lo[:, at], 1, 0)
        cp[level] = part[:R] + part[R:]
    for s in loads[4:]:
        s.wait()
    alpha = scal[0]
    base = 1.0 / (1.0 + 0.25 * wcode[...].astype(f32))
    weight_a = jnp.where(rcode[...] != 2, base, 0.0)
    weight_b = jnp.where(rcode[...] != 1, base, 0.0)
    loads[1].wait()
    for k in range(K):
        at = slice(k * R, (k + 1) * R)
        hi, lo = table(pb, k, R)
        tb_hi[at, :], tb_lo[at, :] = hi, lo
        for source, dest in ((hi, to_hi), (lo, to_lo)):
            dest[at, :] = jnp.concatenate([source[:, (2 * i + 1) * R : (2 * i + 2) * R] for i in range(4)], axis=1)

    part = dot(tb_hi[...], src_c[...], 0, 0) + dot(tb_lo[...], src_c[...], 0, 0)
    part = part[:, :W] + part[:, W:]
    for level in range(9):
        block = part[level * R : (level + 1) * R]
        if level % 2:
            odd[level // 2] = block
        else:
            even[level // 2] = block
    square_a[...] = weight_a * weight_a

    pl.semaphore_wait(barrier, len(peers))
    s_r1 = copy(odd, r1, core())
    s_r1.start()
    s_c1 = [copy(cp.at[d], c1.at[d], along_y(d)) for d in (2, 1, 3)]
    for s in s_c1:
        s.start()
    s_k1 = copy(square_a, next_square_a, far(3))
    pl.when(h > 0)(s_k1.start)

    s_r1.wait_recv()
    for i in range(4):
        even[1 - c + i] = even[1 - c + i] + r1[i]
    s_r2 = []
    for d in (1, 2, 3):
        inside = z + d < 4
        near = copy(even.at[d], r2.at[d], run(d))
        cross = copy(even.at[d], r2.at[d], across(d), again=True)
        pl.when(inside)(near.start)
        pl.when(jnp.logical_not(inside) & (x < 3))(cross.start)
        s_r2.append((near, (d <= z) | (x > 0), inside | (x < 3)))
    s_r3 = copy(even.at[4], r3, along_x(1))
    pl.when(x < 3)(s_r3.start)

    for s in s_c1:
        s.wait_recv()
    here, there = cp[0], cp[4]
    for d in (1, 2, 3):
        mine = d <= y
        here = here + jnp.where(mine, c1[d], 0.0)
        there = there + jnp.where(mine, 0.0, c1[d])
    beyond = there
    cp[4] = there
    s_c2 = copy(cp.at[4], c2, far(1))
    pl.when(h < 3)(s_c2.start)
    part_a = weight_a * (weight_a * here - alpha * resid_a[...])
    cp[0] = part_a
    s_d1 = copy(cp.at[0], next_a, far(3))
    pl.when(h > 0)(s_d1.start)

    rows_here = even[0]
    for d, (s, comes, _) in enumerate(s_r2, 1):
        pl.when(comes)(s.wait_recv)
        rows_here = rows_here + jnp.where(comes, r2[d], 0.0)
    pl.when(x > 0)(s_r3.wait_recv)
    rows_here = rows_here + jnp.where(x > 0, r3[...], 0.0)
    rb = weight_b * rows_here - alpha * resid_b[...]
    wb = weight_b * rb
    ext_e[0] = wb
    s_a2 = []
    for d in (3, 2, 1):
        inside = z + d >= 4
        near = copy(ext_e.at[0], ext_e.at[4 - d], run(d))
        cross = copy(ext_e.at[0], ext_e.at[4 - d], across(d), again=True)
        pl.when(inside)(near.start)
        pl.when(jnp.logical_not(inside) & (x > 0))(cross.start)
        s_a2.append((near, (z + 4 - d < 4) | (x < 3), inside | (x > 0)))
    s_a1 = copy(ext_e.at[0], ext_e.at[4], along_x(3))
    pl.when(x > 0)(s_a1.start)
    raw_b[...] = rb

    pl.when(h > 0)(s_c2.wait_recv)
    came = jnp.where(h > 0, c2[...], 0.0)
    wa = part_a + square_a[...] * came
    ext_c[0] = wa
    s_d2 = []
    for d in (1, 2, 3):
        to = along_y(d)
        s = copy(ext_c.at[0], ext_c.at[4 - d], to)
        later = copy(ext_c.at[4], ext_c.at[4 - d], to, again=True)
        s_d2.append((s, later, y + d >= 4))
    for s, later, now in s_d2:
        pl.when(now)(s.start)
    ra = weight_a * (here + came) - alpha * resid_a[...]
    raw_a[...] = ra
    pl.when(h < 3)(s_k1.wait_recv)
    pl.when(h < 3)(s_d1.wait_recv)
    ext_c[4] = jnp.where(h < 3, next_a[...] + next_square_a[...] * beyond, 0.0)
    for s, later, now in s_d2:
        pl.when(jnp.logical_not(now))(later.start)
    for d in (1, 2, 3):
        pl.semaphore_signal(ready, inc=1, device_id=run(d), device_id_type=MESH)

    def tile_of(q):
        t = jnp.sum(q.reshape(-1, 8, W), axis=0)
        t = t + pltpu.roll(t, 64, 1)
        return t + pltpu.roll(t, 32, 1)

    rr = tile_of(ra * ra + rb * rb)
    sq = jnp.zeros((R, W), f32)
    for k in range(K):
        sq = sq + basis[k] * basis[k]
    vv = tile_of(sq)

    def put_a(level, block):
        hi, lo = split(block)
        wext_a[0:R, level * W : (level + 1) * W] = hi
        wext_a[R : 2 * R, level * W : (level + 1) * W] = lo

    def put_b(level, block):
        hi, lo = split(block)
        wext_b[level * R : (level + 1) * R, 0:W] = hi
        wext_b[level * R : (level + 1) * R, W : 2 * W] = lo

    put_a(0, wa)
    put_a(4, ext_c[4])
    put_b(0, wb)
    for level in (1, 3, 5, 7, 9):
        wext_b[level * R : (level + 1) * R, :] = jnp.zeros((R, 2 * W), bf16)

    ends = wext_a[:, :W], wext_a[:, EXT - W :]
    tables = ta_hi, ta_lo
    ga = sum(dot(w, t[:, at], 1, 1) for t in tables for w, at in zip(ends, (slice(0, W), slice(EXT - W, EXT))))
    ga = ga[:R] + ga[R:]
    for k in range(K):
        raw_v[k] = ga[:, k * W : (k + 1) * W]
    for level, (s, comes, _) in enumerate(s_a2, 1):
        pl.when(comes)(s.wait_recv)
        ext_e[level] = jnp.where(comes, ext_e[level], 0.0)
    pl.when(x < 3)(s_a1.wait_recv)
    ext_e[4] = jnp.where(x < 3, ext_e[4], 0.0)
    s_a3 = copy(ext_e.at[pl.ds(1 - c, 4)], ext_o, core())
    s_a3.start()
    for d in (1, 2, 3, 4):
        put_b(2 * d, ext_e[d])
    gb = dot(tb_hi[...], wext_b[...], 1, 0) + dot(tb_lo[...], wext_b[...], 1, 0)
    gb = gb[:, :W] + gb[:, W:]
    for k in range(K):
        raw_v[k] = raw_v[k] + gb[k * R : (k + 1) * R]
    s_a3.wait_recv()
    for d in range(4):
        hi, lo = split(ext_o[d])
        wext_o[d * R : (d + 1) * R, 0:W] = hi
        wext_o[d * R : (d + 1) * R, W : 2 * W] = lo
    gb = dot(to_hi[...], wext_o[...], 1, 0) + dot(to_lo[...], wext_o[...], 1, 0)
    gb = gb[:, :W] + gb[:, W:]
    for k in range(K):
        raw_v[k] = raw_v[k] + gb[k * R : (k + 1) * R]
    for d, (s, _, _) in enumerate(s_d2, 1):
        s.wait_recv()
        put_a(4 - d, ext_c[4 - d])
    ga = dot(wext_a[:, middle], ta_hi[:, middle], 1, 1)
    ga = ga[:R] + ga[R:] + dot(wext_a[0:R, middle], ta_lo[:, middle], 1, 1)
    zz = jnp.zeros((R, W), f32)
    zv = jnp.zeros((R, W), f32)
    for k in range(K):
        g = m * (raw_v[k] + ga[:, k * W : (k + 1) * W])
        raw_v[k] = g
        zz = zz + g * g
        zv = zv + g * basis[k]

    stores = [(raw_v, raw_v_h), (raw_a, raw_a_h), (raw_b, raw_b_h), (coef, coef_h)]
    stores = [pltpu.make_async_copy(a, b, load_sem.at[i]) for i, (a, b) in enumerate(stores)]

    quarter = lax.broadcasted_iota(jnp.int32, (8, W), 1) // (W // 4)
    both = jnp.where(quarter == 0, rr, vv)
    tile = jnp.where(quarter == 2, tile_of(zz), jnp.where(quarter == 3, tile_of(zv), both))
    sums_plane[0:1, :] = jnp.sum(tile, axis=0, keepdims=True)
    group_plane = share(sums_plane, PLANE, plane, 0)
    for s in stores[:3]:
        s.start()
    sent = {id(s_c2): h < 3, id(s_r3): x < 3, id(s_d1): h > 0, id(s_a1): x > 0, id(s_k1): h > 0}
    sent.update((id(s), goes) for s, _, goes in s_r2 + s_a2)
    for s in started:
        pl.when(sent.get(id(s), True))(s.wait_send)
    group_plane.wait_recv()
    sums_line[0:1, :] = jnp.sum(sums_plane[...], axis=0, keepdims=True)
    pl.semaphore_wait(ready, 3)
    group_line = share(sums_line, LINE, line, 2)
    group_plane.wait_send()
    for s in stores[:3]:
        s.wait()
    group_line.wait_recv()
    row = jnp.sum(sums_line[...], axis=0, keepdims=True)
    mine = quarter == lax.broadcasted_iota(jnp.int32, (8, W), 0)
    sums = jnp.sum(jnp.where(mine, row, 0.0), axis=1, keepdims=True)
    phibar, rhobar = scal[1], scal[2]
    beta_square = sums[0:1] + EPS
    inv_beta = lax.rsqrt(beta_square)
    inv_rho_square = 1.0 / (rhobar * rhobar + beta_square)
    beta = beta_square * inv_beta
    alpha_square = sums[2:3] * (inv_beta * inv_beta) - 2.0 * sums[3:4] + beta_square * sums[1:2] + EPS
    inv_alpha = lax.rsqrt(alpha_square)
    alpha_next = alpha_square * inv_alpha
    step = rhobar * phibar * inv_rho_square
    values = (inv_beta, inv_beta * inv_alpha, beta * inv_alpha, step, beta * alpha_next * inv_rho_square)
    for i, value in enumerate(values):
        coef[i : i + 1, :] = jnp.broadcast_to(value, (1, W))
    coef[5:8, :] = jnp.zeros((3, W), f32)
    stores[3].start()
    group_line.wait_send()
    stores[3].wait()


N_COPIES = 19


def finish(
    grad_h, raw_a_h, raw_b_h, coef_h, sol_h, search_h, basis_h,
    sol_o, search_o, basis_o, resid_a_o, resid_b_o,
    grad, raw_a, raw_b, coef, sol, search, basis, load_sem, store_sem,
):
    pairs = (
        (coef_h, coef), (search_h, search), (sol_h, sol), (grad_h, grad), (basis_h, basis), (raw_a_h, raw_a), (raw_b_h, raw_b),
    )
    loads = [pltpu.make_async_copy(a, b, load_sem.at[i]) for i, (a, b) in enumerate(pairs)]
    for s in loads:
        s.start()
    pairs = ((sol, sol_o), (grad, basis_o), (search, search_o), (raw_a, resid_a_o), (raw_b, resid_b_o))
    stores = [pltpu.make_async_copy(a, b, store_sem.at[i]) for i, (a, b) in enumerate(pairs)]
    for s in loads[:3]:
        s.wait()
    inv_beta, scale, shift = coef[0:1, :], coef[1:2, :], coef[2:3, :]
    step, turn = coef[3:4, :], coef[4:5, :]
    sol[...] = sol[...] + step * search[...]
    stores[0].start()
    for s in loads[3:5]:
        s.wait()
    v = grad[...] * scale - shift * basis[...]
    grad[...] = v
    stores[1].start()
    search[...] = v - turn * search[...]
    stores[2].start()
    for s in loads[5:]:
        s.wait()
    raw_a[...] = raw_a[...] * inv_beta
    stores[3].start()
    raw_b[...] = raw_b[...] * inv_beta
    stores[4].start()
    for s in stores:
        s.wait()


def body(sol, search, basis, resid_a, resid_b, scal, pa, pb, mask, wcode, rcode):
    hbm = pl.BlockSpec(memory_space=pltpu.HBM)
    image = jax.ShapeDtypeStruct((R, W), f32)
    maps = jax.ShapeDtypeStruct((K, R, W), f32)
    words = pltpu.VMEM((R, W), jnp.int32)
    outs = pl.pallas_call(
        kernel,
        out_shape=(maps, image, image, jax.ShapeDtypeStruct((8, W), f32)),
        in_specs=[hbm] * 9,
        out_specs=(hbm,) * 4,
        scratch_shapes=[
            pltpu.VMEM((K, R, W), f32),
            pltpu.VMEM((R, W), f32),
            pltpu.VMEM((R, W), f32),
            pltpu.VMEM((8, W), f32),
            pltpu.VMEM((K, R, W), f32),
            pltpu.VMEM((R, W), f32),
            pltpu.VMEM((R, W), f32),
            pltpu.SMEM((3,), f32),
            pltpu.VMEM((K, L), f32),
            pltpu.VMEM((K, L), f32),
            words,
            words,
            words,
            pltpu.VMEM((2 * R, K * W), bf16),
            pltpu.VMEM((K * R, 2 * W), bf16),
            pltpu.VMEM((K * W, EXT), bf16),
            pltpu.VMEM((K * W, EXT), bf16),
            pltpu.VMEM((K * R, EXT), bf16),
            pltpu.VMEM((K * R, EXT), bf16),
            pltpu.VMEM((K * R, 4 * R), bf16),
            pltpu.VMEM((K * R, 4 * R), bf16),
            pltpu.VMEM((2 * R, EXT), bf16),
            pltpu.VMEM((EXT, 2 * W), bf16),
            pltpu.VMEM((4 * R, 2 * W), bf16),
            pltpu.VMEM((5, R, W), f32),
            pltpu.VMEM((4, R, W), f32),
            pltpu.VMEM((4, R, W), f32),
            pltpu.VMEM((4, R, W), f32),
            pltpu.VMEM((R, W), f32),
            pltpu.VMEM((5, R, W), f32),
            pltpu.VMEM((4, R, W), f32),
            pltpu.VMEM((R, W), f32),
            pltpu.VMEM((5, R, W), f32),
            pltpu.VMEM((5, R, W), f32),
            pltpu.VMEM((4, R, W), f32),
            pltpu.VMEM((1 + len(PLANE), W), f32),
            pltpu.VMEM((1 + len(LINE), W), f32),
            pltpu.SemaphoreType.DMA((N_COPIES,)),
            pltpu.SemaphoreType.DMA((N_COPIES,)),
            pltpu.SemaphoreType.DMA((4,)),
            pltpu.SemaphoreType.DMA((9,)),
            pltpu.SemaphoreType.REGULAR,
            *[pltpu.VMEM((R, W), f32)] * 3,
        ],
        compiler_params=pltpu.CompilerParams(
            collective_id=0, has_side_effects=True, vmem_limit_bytes=56 * 1024 * 1024
        ),
    )(basis, resid_a, resid_b, scal, pa, pb, mask, wcode, rcode)
    return pl.pallas_call(
        finish,
        out_shape=(maps, maps, maps, image, image),
        in_specs=[hbm] * 7,
        out_specs=(hbm,) * 5,
        scratch_shapes=[
            pltpu.VMEM((K, R, W), f32),
            pltpu.VMEM((R, W), f32),
            pltpu.VMEM((R, W), f32),
            pltpu.VMEM((8, W), f32),
            pltpu.VMEM((K, R, W), f32),
            pltpu.VMEM((K, R, W), f32),
            pltpu.VMEM((K, R, W), f32),
            pltpu.SemaphoreType.DMA((7,)),
            pltpu.SemaphoreType.DMA((5,)),
        ],
        compiler_params=pltpu.CompilerParams(vmem_limit_bytes=56 * 1024 * 1024),
    )(*outs, sol, search, basis)


def solution(mesh):
    torus = Mesh(mesh.devices.reshape(4, 4, 2, 4, 4), (X, Z, C, H, Y))
    maps, image = P(None, ROW, COL), P(ROW, COL)
    return jax.shard_map(
        body,
        mesh=torus,
        in_specs=(maps, maps, maps, image, image, P(), P(), P(), image, image, image),
        out_specs=(maps, maps, maps, image, image),
        check_vma=False,
    )
```
